128 devices in a mesh: row: 8 (over x, y_lo), col: 16 (over y_hi, z, core).
Axes of the slice: x: 4, y: 4 (y_hi: 2, y_lo: 2; y = y_hi * 2 + y_lo), z: 4, core: 2. Of those that a mesh axis runs over, the one named last changes fastest.
Arguments:
- momentum: float32 [29568, 8192], P(('row', 'col')), may hold values from -100 to 100
- gradient: bfloat16 [29568, 8192], P(('row', 'col')), may hold values from -24 to 24
- right_basis: bfloat16 [8192, 512], P(('row', 'col')), may hold values from -0.0625 to 0.0625
- weight: bfloat16 [29568, 8192], P('row', 'col'), may hold values from -6 to 6
- tokens: bfloat16 [512, 29568], P('col', 'row'), may hold values from -6 to 6
Outputs:
- new_momentum: float32 [29568, 8192], P(('row', 'col'))
- new_basis: bfloat16 [8192, 512], P(('row', 'col'))
- new_weight: bfloat16 [29568, 8192], P('row', 'col')
- logits: bfloat16 [512, 8192], P('row', 'col')
The draws below stay inside these ranges and needn't reach their ends.
All inputs are finite; a program needn't handle non-finite values.
Results may differ from the reference program's by a relative error of at most 0.02.
Values may be sent and summed in bfloat16 or wider, within the bound.
No kernel may reach another device: no remote copies, remote signals or barrier semaphores. Data moves between devices by JAX's collectives and lax.ppermute only.
A program may use at most 128 MiB of HBM per device.

```python
import math
import jax
import jax.numpy as jnp
from jax import lax

D = 8192
FF = 29568
RANK = 512
BATCH = 512


def draw_momentum(key, part):
    key = jax.random.fold_in(key, 17)
    keys = jax.random.split(key, 3)
    row_ramp = jnp.arange(FF, dtype=jnp.float32) / FF
    col_ramp = jnp.arange(D, dtype=jnp.float32) / D
    row_scale = jnp.exp(jax.random.uniform(keys[0], (FF,), jnp.float32, -1.15, 1.15) + 0.55 * row_ramp - 0.275)
    col_scale = jnp.exp(jax.random.uniform(keys[1], (D,), jnp.float32, -1.15, 1.15) + 0.55 * col_ramp - 0.275)
    values = jax.random.truncated_normal(keys[2], -5.0, 5.0, (FF, D), jnp.float32)
    return values * row_scale[:, None] * col_scale[None, :]


def spiked(array, rng, source, target, blocks, factor):
    owner, partner = [(jnp.arange(array.shape[dim]) // (array.shape[dim] // blocks)).reshape([-1 if axis == dim else 1 for axis in range(array.ndim)]) for dim in (source, target)]
    chosen = jax.random.permutation(rng, blocks)[partner]
    strong = (owner == chosen) | (owner == (partner + blocks // 2) % blocks)
    return jnp.where(strong, factor * array, array)


def shard_levels(stream_key, shape, shards, smallest, top_value):
    def one(dim, shards_of):
        draws = jax.random.uniform(jax.random.fold_in(jax.random.fold_in(stream_key, 6), dim), (shards_of,), jnp.float32, smallest / len(shards), top_value / len(shards))
        return jnp.repeat(jnp.exp(draws), shape[dim] // shards_of).reshape((-1,) + (1,) * (len(shape) - dim - 1))

    loudness = one(*shards[0])
    for cut in shards[1:]:
        loudness = loudness * one(*cut)
    return loudness


def normal_values(stream_key, dims, spread, limit, cuts=(), held_as=jnp.bfloat16):
    entries = jax.random.normal(stream_key, dims, jnp.float32) * spread
    if len(cuts) > 0:
        entries = shard_levels(stream_key, dims, cuts, -0.22, 0.18) * entries
    return jnp.clip(entries, min=-limit, max=limit).astype(held_as)


def gaussian_with(own_key, shape, spread, most, cuts, heavy, kind=jnp.bfloat16):
    values = spread * jax.random.normal(own_key, shape, jnp.float32)
    if cuts:
        values = values * shard_levels(own_key, shape, cuts, -0.22, 0.18)
    return jnp.clip(spiked(values, jax.random.fold_in(own_key, 3), *heavy), -most, most).astype(kind)


def setup_inputs(seed: int = 0) -> dict:
    arg_keys = jax.random.split(jax.random.key(seed), 6)
    return {
        "momentum": draw_momentum(jax.random.fold_in(arg_keys[5], 71), 0),
        "gradient": gaussian_with(arg_keys[1], (FF, D), 1.0, 24.0, ((0, 128),), (0, 1, 128, 5.5)),
        "right_basis": normal_values(arg_keys[2], (D, RANK), D ** -0.5, 0.0625, ((0, 128),)),
        "weight": normal_values(arg_keys[3], (FF, D), 1.0, 6.0, ((0, 8), (1, 16))),
        "tokens": normal_values(arg_keys[4], (BATCH, FF), 1.0, 6.0, ((0, 16), (1, 8))),
    }


EPSILON = 1e-06
MOMENTUM_DECAY = 0.95
STEP_SIZE = 0.3

def contract_rows(left, right):
    return lax.dot_general(left.astype(jnp.float32), right.astype(jnp.float32), (((0,), (0,)), ((), ())))

def contract_cols(left, right):
    return lax.dot_general(left.astype(jnp.float32), right.astype(jnp.float32), (((1,), (1,)), ((), ())))

def reference(momentum, gradient, right_basis, weight, tokens):
    buffer = momentum + gradient.astype(jnp.float32)
    buffer_low = buffer.astype(jnp.bfloat16)
    projected = jnp.dot(buffer_low, right_basis, preferred_element_type=jnp.float32)
    left_factor = (projected * lax.rsqrt(lax.optimization_barrier(jnp.sum(projected * projected, axis=0)) + EPSILON)).astype(jnp.bfloat16)
    back_low = contract_rows(buffer_low, left_factor).astype(jnp.bfloat16)
    back_wide = back_low.astype(jnp.float32)
    new_basis = (back_wide * lax.rsqrt(lax.optimization_barrier(jnp.sum(back_wide * back_wide, axis=0)) + EPSILON)).astype(jnp.bfloat16)
    step_scale = STEP_SIZE * math.sqrt(FF * D / RANK)
    blocks_count = 16

    def momentum_block(pieces):
        return pieces[0] - (1.0 - MOMENTUM_DECAY) * contract_cols(pieces[1], back_low)

    def weight_block(pieces):
        change = contract_cols(pieces[1], new_basis)
        return (pieces[0].astype(jnp.float32) - step_scale * change).astype(jnp.bfloat16)
    factor_blocks = left_factor.reshape(blocks_count, FF // blocks_count, RANK)
    new_momentum = lax.map(momentum_block, (buffer.reshape(blocks_count, FF // blocks_count, D), factor_blocks)).reshape(FF, D)
    new_weight = lax.map(weight_block, (weight.reshape(blocks_count, FF // blocks_count, D), factor_blocks)).reshape(FF, D)
    summed_logits = jnp.dot(tokens, new_weight, preferred_element_type=jnp.float32)
    logits = (summed_logits * FF ** (-0.5)).astype(jnp.bfloat16)
    return (new_momentum, new_basis, new_weight, logits)
```

```python
import math

import jax
import jax.numpy as jnp
from jax import lax
from jax.experimental import pallas as pl
from jax.experimental.pallas import tpu as pltpu
from jax.sharding import PartitionSpec as P

EPSILON = 1e-06
MOMENTUM_DECAY = 0.95
STEP_SIZE = 0.3
BF = jnp.bfloat16
F32 = jnp.float32
ALL = ("row", "col")
VMEM_LIMIT = 48 * 1024 * 1024
HALF = 256
UNIT = 512


def device_id(x, y, z, core):
    x, y, z = x % 4, y % 4, z % 4
    return (x * 2 + y % 2) * 16 + (y // 2) * 8 + z * 2 + core


def places():
    return [(x, y, z, c) for x in range(4) for y in range(4) for z in range(4) for c in range(2)]


def moved(place, axis, shift):
    place = list(place)
    place["xyz".index(axis)] += shift
    return device_id(*place)


def shift_by(value, axes, shift):
    pairs = [(device_id(*p), moved(p, axes[p[3]], shift)) for p in places()]
    return lax.ppermute(value, ALL, pairs)


def swap_cores(value):
    return lax.ppermute(value, ALL, [(i, i ^ 1) for i in range(128)])


def gather_ring(block, axes):
    after = shift_by(block, axes, -1)
    before = shift_by(block, axes, 1)
    across = shift_by(block, axes, 2)
    return [block, after, across, before]


def scatter_ring(blocks, axes):
    from_before = shift_by(blocks[1], axes, 1)
    from_after = shift_by(blocks[3], axes, -1)
    from_across = shift_by(blocks[2], axes, 2)
    return (
        (blocks[0].astype(F32) + from_across.astype(F32))
        + (from_before.astype(F32) + from_after.astype(F32))
    )


def rotate(stack, start):
    return lax.dynamic_slice_in_dim(jnp.concatenate([stack, stack], 0), start, 4, 0)


def params():
    return pltpu.CompilerParams(vmem_limit_bytes=VMEM_LIMIT)


def project(order, own, other, pieces):
    rows = own.shape[0]

    def kernel(order_ref, own_ref, other_ref, r0, r1, r2, r3, out_own, out_other, squares, acc):
        step = pl.program_id(0)

        @pl.when(step == 0)
        def _():
            acc[...] = jnp.zeros_like(acc)

        for k, ref in enumerate((r0, r1, r2, r3)):

            @pl.when(step // 4 == k)
            def _(ref=ref):
                acc[0] += jnp.dot(own_ref[...], ref[0], preferred_element_type=F32)
                acc[1] += jnp.dot(other_ref[...], ref[0], preferred_element_type=F32)

        @pl.when(step == 15)
        def _():
            out_own[...] = acc[0]
            out_other[...] = acc[1].astype(BF)
            squares[...] = jnp.sum(acc[0] * acc[0] + acc[1] * acc[1], axis=0, keepdims=True)

    def piece_spec(k):
        return pl.BlockSpec(
            (1, UNIT, HALF), lambda i, order: (jnp.clip(i - 4 * k, 0, 3), 0, 0)
        )

    column = pl.BlockSpec((rows, UNIT), lambda i, order: (0, order[i]))
    whole = lambda shape: pl.BlockSpec(shape, lambda i, order: (0, 0))
    return pl.pallas_call(
        kernel,
        grid_spec=pltpu.PrefetchScalarGridSpec(
            num_scalar_prefetch=1,
            grid=(16,),
            in_specs=[column, column] + [piece_spec(k) for k in range(4)],
            out_specs=[whole((rows, HALF)), whole((rows, HALF)), whole((1, HALF))],
            scratch_shapes=[pltpu.VMEM((2, rows, HALF), F32)],
        ),
        out_shape=[
            jax.ShapeDtypeStruct((rows, HALF), F32),
            jax.ShapeDtypeStruct((rows, HALF), BF),
            jax.ShapeDtypeStruct((1, HALF), F32),
        ],
        compiler_params=params(),
    )(order, own, other, *pieces)


def project_back(order, own, other, p_own, p_other):
    rows = own.shape[0]
    contract = (((0,), (0,)), ((), ()))

    def kernel(order_ref, own_ref, other_ref, p_own_ref, p_other_ref, q0, q1, q2, q3):
        step = pl.program_id(0)
        value = lax.dot_general(p_own_ref[...], own_ref[...], contract, preferred_element_type=F32)
        value += lax.dot_general(
            p_other_ref[...], other_ref[...], contract, preferred_element_type=F32
        )
        value = value.astype(BF)
        for k, ref in enumerate((q0, q1, q2, q3)):

            @pl.when(step // 4 == k)
            def _(ref=ref):
                ref[0] = value

    column = pl.BlockSpec((rows, UNIT), lambda i, order: (0, order[i]))
    whole = pl.BlockSpec((rows, HALF), lambda i, order: (0, 0))

    def slab_spec(k):
        return pl.BlockSpec(
            (1, HALF, UNIT), lambda i, order: (jnp.clip(i - 4 * k, 0, 3), 0, 0)
        )

    return pl.pallas_call(
        kernel,
        grid_spec=pltpu.PrefetchScalarGridSpec(
            num_scalar_prefetch=1,
            grid=(16,),
            in_specs=[column, column, whole, whole],
            out_specs=[slab_spec(k) for k in range(4)],
        ),
        out_shape=[jax.ShapeDtypeStruct((4, HALF, UNIT), BF)] * 4,
        compiler_params=params(),
    )(order, own, other, p_own, p_other)


def update_momentum(where_own, where_other, momentum, gradient, left_own, left_other, q_own, q_other):
    rows, width = momentum.shape

    def kernel(a_ref, b_ref, m_ref, g_ref, lo_ref, lp_ref, qo_ref, qp_ref, out_ref):
        change = jnp.dot(lo_ref[...], qo_ref[0], preferred_element_type=F32)
        change += jnp.dot(lp_ref[...], qp_ref[0], preferred_element_type=F32)
        out_ref[...] = (m_ref[...] + g_ref[...].astype(F32)) - change

    column = pl.BlockSpec((rows, UNIT), lambda i, a, b: (0, i))
    whole = pl.BlockSpec((rows, HALF), lambda i, a, b: (0, 0))
    return pl.pallas_call(
        kernel,
        grid_spec=pltpu.PrefetchScalarGridSpec(
            num_scalar_prefetch=2,
            grid=(16,),
            in_specs=[
                column,
                column,
                whole,
                whole,
                pl.BlockSpec((1, HALF, UNIT), lambda i, a, b: (a[i], 0, 0)),
                pl.BlockSpec((1, HALF, UNIT), lambda i, a, b: (b[i], 0, 0)),
            ],
            out_specs=column,
        ),
        out_shape=jax.ShapeDtypeStruct((rows, width), F32),
        compiler_params=params(),
    )(where_own, where_other, momentum, gradient, left_own, left_other, q_own, q_other)


def shards(momentum, gradient, right_basis, weight, tokens):
    row, col = lax.axis_index("row"), lax.axis_index("col")
    x, y, z, core = row // 2, (col // 8) * 2 + row % 2, (col // 2) % 4, col % 2
    first = core == 0
    total_rows = momentum.shape[0] * 128
    rank = right_basis.shape[1]
    width = momentum.shape[1]
    big, middle = ("x", "y"), ("y", "x")
    deep = ("z", "z")

    i = jnp.arange(16, dtype=jnp.int32)

    def unit_at(core_is_first):
        far, near = i // 4, i % 4
        ux = jnp.where(core_is_first, x + far, x + near) % 4
        uy = jnp.where(core_is_first, y + near, y + far) % 4
        return (ux * 4 + (uy % 2) * 2 + uy // 2).astype(jnp.int32)

    def place_of(core_is_first):
        ux, uy = i // 4, (i % 2) * 2 + (i // 2) % 2
        dx, dy = (ux - x) % 4, (uy - y) % 4
        return jnp.where(core_is_first, dx * 4 + dy, dy * 4 + dx).astype(jnp.int32)

    order = unit_at(first)
    where_own, where_other = place_of(first), place_of(jnp.logical_not(first))

    def halves(a):
        low, high = a[:, :HALF], a[:, HALF:]
        return jnp.where(first, low, high), jnp.where(first, high, low)

    def by_core(mine, theirs):
        return jnp.where(first, mine, theirs), jnp.where(first, theirs, mine)

    basis_own, basis_sent = halves(right_basis)
    basis_chip = jnp.concatenate(by_core(basis_own, swap_cores(basis_sent)), 0)
    stack = jnp.stack(gather_ring(basis_chip, deep))
    unit = rotate(stack, (4 - z) % 4).reshape(UNIT, HALF)
    slab = jnp.stack(gather_ring(unit, middle))
    pieces = gather_ring(slab, big)

    buffer_low = (momentum + gradient.astype(F32)).astype(BF)
    buffer_other = swap_cores(buffer_low)
    tokens_all = lax.all_gather(tokens, "col", axis=0, tiled=True)

    p_own, p_other, squares = project(order, buffer_low, buffer_other, pieces)
    p_own_low = p_own.astype(BF)
    p_from_other = swap_cores(p_other)

    p_tile = lax.all_gather(jnp.stack(by_core(p_own_low, p_other)), "col", axis=0,
                            axis_index_groups=[[c + 2 * k for k in range(8)] for c in range(2)], tiled=True)
    p_tile = p_tile.reshape(-1, HALF)
    p_tile_other = swap_cores(p_tile)

    slabs = project_back(order, buffer_low, buffer_other, p_own_low, p_other)
    chips = [[2 * k + c for k in range(64)] for c in range(2)]

    def total(part):
        parts = lax.all_to_all(jnp.broadcast_to(part[None], (64, 1, HALF)), ALL, 0, 0,
                               axis_index_groups=chips, tiled=True)
        return jnp.sum(parts, axis=(0, 1))

    p_squares = total(squares)
    scale = lax.rsqrt(p_squares + EPSILON)
    summed = scatter_ring(slabs, big).astype(BF)
    summed = scatter_ring([summed[k] for k in range(4)], middle).astype(BF)
    summed = summed.reshape(HALF, 4, 128).transpose(1, 0, 2)
    summed = rotate(summed, z)
    q_block = scatter_ring([summed[k] for k in range(4)], deep).astype(BF)

    q_wide = q_block.astype(F32)
    q_squares = total(jnp.sum(q_wide * q_wide, axis=1)[None])
    stack = rotate(jnp.stack(gather_ring(q_block, deep)), (4 - z) % 4)
    unit = stack.transpose(1, 0, 2).reshape(HALF, UNIT)
    slab = jnp.stack(gather_ring(unit, middle))
    q_own = jnp.concatenate(gather_ring(slab, big), 0)
    q_other = swap_cores(q_own)

    basis_scale = lax.rsqrt(scale * scale * q_squares + EPSILON)
    scales = jnp.stack([scale, basis_scale])
    scales_other = swap_cores(scales)

    factor = 1.0 - MOMENTUM_DECAY
    left_own = (p_own * (factor * scale * scale)).astype(BF)
    left_other = (p_from_other.astype(F32) * (factor * scales_other[0] * scales_other[0])).astype(BF)
    new_momentum = update_momentum(
        where_own, where_other, momentum, gradient, left_own, left_other, q_own, q_other
    )

    basis_block = q_wide * (scale * basis_scale)[:, None]
    low, high = basis_block[:, :64], basis_block[:, 64:]
    mine = jnp.where(first, low, high).T.astype(BF)
    theirs = jnp.where(first, high, low).T.astype(BF)
    new_basis = jnp.concatenate(by_core(mine, swap_cores(theirs)), 1)

    step_scale = STEP_SIZE * math.sqrt(total_rows * width / rank)
    tile_own = lax.dynamic_index_in_dim(q_own, where_own[col], 0, keepdims=False).astype(F32)
    tile_other = lax.dynamic_index_in_dim(q_other, where_other[col], 0, keepdims=False).astype(F32)
    tile_own = (tile_own * (step_scale * scale * scale * basis_scale)[:, None]).astype(BF)
    tile_other = (
        tile_other * (step_scale * scales_other[0] * scales_other[0] * scales_other[1])[:, None]
    ).astype(BF)
    change = jnp.dot(p_tile, tile_own, preferred_element_type=F32) + jnp.dot(
        p_tile_other, tile_other, preferred_element_type=F32
    )
    new_weight = (weight.astype(F32) - change).astype(BF)

    early = jnp.concatenate(
        [
            jnp.dot(tokens_all, weight, preferred_element_type=F32),
            jnp.dot(tokens_all, p_tile, preferred_element_type=F32),
            jnp.dot(tokens_all, p_tile_other, preferred_element_type=F32),
        ],
        1,
    )
    early = lax.psum_scatter(early, "row", scatter_dimension=0, tiled=True)
    tokens_left = early[:, UNIT:].astype(BF)
    late = jnp.dot(tokens_left[:, :HALF], tile_own, preferred_element_type=F32) + jnp.dot(
        tokens_left[:, HALF:], tile_other, preferred_element_type=F32
    )
    logits = ((early[:, :UNIT] - late) * total_rows ** (-0.5)).astype(BF)
    return (new_momentum, new_basis, new_weight, logits)


def solution(mesh):
    in_specs = (
        P(("row", "col"), None),
        P(("row", "col"), None),
        P(("row", "col"), None),
        P("row", "col"),
        P("col", "row"),
    )
    out_specs = (P(("row", "col"), None), P(("row", "col"), None), P("row", "col"), P("row", "col"))
    return jax.shard_map(shards, mesh=mesh, in_specs=in_specs, out_specs=out_specs, check_vma=False)
```

```python
import math

import jax
import jax.numpy as jnp
from jax import lax
from jax.experimental import pallas as pl
from jax.experimental.pallas import tpu as pltpu
from jax.sharding import PartitionSpec as P

EPSILON = 1e-06
MOMENTUM_DECAY = 0.95
STEP_SIZE = 0.3
BF = jnp.bfloat16
F32 = jnp.float32
ALL = ("row", "col")
VMEM_LIMIT = 48 * 1024 * 1024
HALF = 256
UNIT = 512


def device_id(x, y, z, core):
    x, y, z = x % 4, y % 4, z % 4
    return (x * 2 + y % 2) * 16 + (y // 2) * 8 + z * 2 + core


def places():
    return [(x, y, z, c) for x in range(4) for y in range(4) for z in range(4) for c in range(2)]


def moved(place, axis, shift):
    place = list(place)
    place["xyz".index(axis)] += shift
    return device_id(*place)


def shift_by(value, axes, shift):
    pairs = [(device_id(*p), moved(p, axes[p[3]], shift)) for p in places()]
    return lax.ppermute(value, ALL, pairs)


def swap_cores(value):
    return lax.ppermute(value, ALL, [(i, i ^ 1) for i in range(128)])


def gather_ring(block, axes):
    after = shift_by(block, axes, -1)
    before = shift_by(block, axes, 1)
    across = shift_by(block, axes, 2)
    return [block, after, across, before]


def scatter_ring(blocks, axes):
    from_before = shift_by(blocks[1], axes, 1)
    from_after = shift_by(blocks[3], axes, -1)
    from_across = shift_by(blocks[2], axes, 2)
    return (
        (blocks[0].astype(F32) + from_across.astype(F32))
        + (from_before.astype(F32) + from_after.astype(F32))
    )


def rotate(stack, start):
    return lax.dynamic_slice_in_dim(jnp.concatenate([stack, stack], 0), start, 4, 0)


def params():
    return pltpu.CompilerParams(vmem_limit_bytes=VMEM_LIMIT)


def column_specs(rows, count):
    return [
        pl.BlockSpec((rows, UNIT), lambda i, order, u=u: (0, order[4 * i + u])) for u in range(count)
    ]


def project(order, own, other, pieces, sums=None):
    rows = own.shape[0]
    count = len(pieces)
    last = sums is not None

    def kernel(order_ref, *refs):
        own_refs, other_refs, slabs = refs[:4], refs[4:8], refs[8 : 8 + count]
        rest = refs[8 + count :]
        step = pl.program_id(0)

        def part(columns, slab):
            total = jnp.dot(columns[0][...], slab[0], preferred_element_type=F32)
            for u in range(1, 4):
                total += jnp.dot(columns[u][...], slab[u], preferred_element_type=F32)
            return total

        if last:
            mine = rest[0][...] + part(own_refs, slabs[0])
            theirs = rest[1][...] + part(other_refs, slabs[0])
            rest[2][...] = mine
            rest[3][...] = mine.astype(BF)
            rest[4][...] = theirs.astype(BF)
            rest[5][...] = jnp.sum(mine * mine + theirs * theirs, axis=0, keepdims=True)
            return
        for k, slab in enumerate(slabs):

            @pl.when(step == k)
            def _(slab=slab, k=k):
                mine, theirs = part(own_refs, slab), part(other_refs, slab)
                rest[0][...] = mine if k == 0 else rest[0][...] + mine
                rest[1][...] = theirs if k == 0 else rest[1][...] + theirs

    whole = pl.BlockSpec((rows, HALF), lambda i, order: (0, 0))
    slab_spec = pl.BlockSpec((4, UNIT, HALF), lambda i, order: (0, 0, 0))
    shape = lambda dtype: jax.ShapeDtypeStruct((rows, HALF), dtype)
    in_specs = column_specs(rows, 4) * 2 + [slab_spec] * count
    out_specs, out_shape = [whole, whole], [shape(F32), shape(F32)]
    if last:
        in_specs += [whole, whole]
        out_specs = [whole, whole, whole, pl.BlockSpec((1, HALF), lambda i, order: (0, 0))]
        out_shape = [shape(F32), shape(BF), shape(BF), jax.ShapeDtypeStruct((1, HALF), F32)]
    return pl.pallas_call(
        kernel,
        grid_spec=pltpu.PrefetchScalarGridSpec(
            num_scalar_prefetch=1, grid=(count,), in_specs=in_specs, out_specs=out_specs
        ),
        out_shape=out_shape,
        compiler_params=params(),
    )(order, *([own] * 4), *([other] * 4), *pieces, *(sums or ()))


def project_back(order, own, other, p_own, p_other):
    rows = own.shape[0]
    count = order.shape[0] // 4
    contract = (((0,), (0,)), ((), ()))

    def kernel(order_ref, *refs):
        own_refs, other_refs, (p_own_ref, p_other_ref), outs = refs[:4], refs[4:8], refs[8:10], refs[10:]
        step = pl.program_id(0)
        for k, out in enumerate(outs):

            @pl.when(step == k)
            def _(out=out):
                for u in range(4):
                    value = lax.dot_general(
                        p_own_ref[...], own_refs[u][...], contract, preferred_element_type=F32
                    )
                    value += lax.dot_general(
                        p_other_ref[...], other_refs[u][...], contract, preferred_element_type=F32
                    )
                    out[u] = value.astype(BF)

    whole = pl.BlockSpec((rows, HALF), lambda i, order: (0, 0))
    return pl.pallas_call(
        kernel,
        grid_spec=pltpu.PrefetchScalarGridSpec(
            num_scalar_prefetch=1,
            grid=(count,),
            in_specs=column_specs(rows, 4) * 2 + [whole, whole],
            out_specs=[pl.BlockSpec((4, HALF, UNIT), lambda i, order: (0, 0, 0))] * count,
        ),
        out_shape=[jax.ShapeDtypeStruct((4, HALF, UNIT), BF)] * count,
        compiler_params=params(),
    )(order, *([own] * 4), *([other] * 4), p_own, p_other)


def update_momentum(order, units, momentum, gradient, left_own, left_other, q_own, q_other, previous=None):
    rows, width = momentum.shape
    places = sorted({k for k, _ in units} | {j for _, j in units})
    own = {k: q_own[k] for k in places if any(a == k for a, _ in units)}
    other = {j: q_other[j] for j in places if any(b == j for _, b in units)}
    own_at = {k: n for n, k in enumerate(own)}
    other_at = {j: n + len(own) for n, j in enumerate(other)}
    slabs = len(own) + len(other)

    def kernel(order_ref, m_ref, g_ref, lo_ref, lp_ref, *refs):
        step = pl.program_id(0)
        out_ref = refs[-1]
        for n, (k, j) in enumerate(units):

            @pl.when(step == n)
            def _(k=k, j=j):
                change = jnp.dot(lo_ref[...], refs[own_at[k]][j], preferred_element_type=F32)
                change += jnp.dot(lp_ref[...], refs[other_at[j]][k], preferred_element_type=F32)
                out_ref[...] = (m_ref[...] + g_ref[...].astype(F32)) - (1.0 - MOMENTUM_DECAY) * change

    column = pl.BlockSpec((rows, UNIT), lambda i, order: (0, order[i]))
    whole = pl.BlockSpec((rows, HALF), lambda i, order: (0, 0))
    slab = pl.BlockSpec((4, HALF, UNIT), lambda i, order: (0, 0, 0))
    in_specs = [column, column, whole, whole] + [slab] * slabs
    operands = [momentum, gradient, left_own, left_other, *own.values(), *other.values()]
    aliases = {}
    if previous is not None:
        in_specs.append(pl.BlockSpec(memory_space=pl.ANY))
        operands.append(previous)
        aliases = {len(operands): 0}
    return pl.pallas_call(
        kernel,
        grid_spec=pltpu.PrefetchScalarGridSpec(
            num_scalar_prefetch=1, grid=(len(units),), in_specs=in_specs, out_specs=column
        ),
        out_shape=jax.ShapeDtypeStruct((rows, width), F32),
        input_output_aliases=aliases,
        compiler_params=params(),
    )(order, *operands)


def three_terms(value):
    high = value.astype(BF)
    rest = value - high.astype(F32)
    middle = rest.astype(BF)
    return jnp.stack([high, middle, (rest - middle.astype(F32)).astype(BF)])


def shards(momentum, gradient, right_basis, weight, tokens):
    row, col = lax.axis_index("row"), lax.axis_index("col")
    x, y, z, core = row // 2, (col // 8) * 2 + row % 2, (col // 2) % 4, col % 2
    first = core == 0
    total_rows = momentum.shape[0] * 128
    rank = right_basis.shape[1]
    width = momentum.shape[1]
    rows = momentum.shape[0]
    big, middle = ("x", "y"), ("y", "x")
    deep = ("z", "z")

    def unit_at(k, j):
        ux = jnp.where(first, x + k, x + j) % 4
        uy = jnp.where(first, y + j, y + k) % 4
        return ux * 4 + (uy % 2) * 2 + uy // 2

    def orders(units):
        return jnp.stack([unit_at(k, j) for k, j in units]).astype(jnp.int32)

    def slab_orders(*slabs):
        return orders([(k, j) for k in slabs for j in range(4)])

    def halves(a):
        low, high = a[:, :HALF], a[:, HALF:]
        return jnp.where(first, low, high), jnp.where(first, high, low)

    def by_core(mine, theirs):
        return jnp.where(first, mine, theirs), jnp.where(first, theirs, mine)

    def by_half(mine, theirs):
        low = y < 2
        return jnp.stack([jnp.where(low, mine, theirs), jnp.where(low, theirs, mine)])

    def swap_y_hi(value):
        return shift_by(value, ("y", "y"), 2)

    basis_own, basis_sent = halves(right_basis)
    basis_other = swap_cores(basis_sent)
    basis_chip = jnp.concatenate(by_core(basis_own, basis_other), 0)
    stack = jnp.stack(gather_ring(basis_chip, deep))
    unit = rotate(stack, (4 - z) % 4).reshape(UNIT, HALF)
    slab = jnp.stack(gather_ring(unit, middle))
    pieces = gather_ring(slab, big)

    buffer_low = (momentum + gradient.astype(F32)).astype(BF)
    buffer_sent, _ = lax.optimization_barrier((buffer_low, basis_other))
    buffer_other = swap_cores(buffer_sent)

    tokens_pair = jnp.concatenate([tokens, swap_y_hi(tokens)], 0)
    tokens_own = jnp.concatenate(gather_ring(tokens_pair, deep), 0)
    tokens_other = swap_cores(tokens_own)

    sums = project(slab_orders(0, 1, 3), buffer_low, buffer_other, [pieces[0], pieces[1], pieces[3]])
    p_own, p_own_low, p_other, p_squares = project(
        slab_orders(2), buffer_low, buffer_other, [pieces[2]], sums
    )

    slabs = [None] * 4
    (slabs[2],) = project_back(slab_orders(2), buffer_low, buffer_other, p_own_low, p_other)
    slabs[1], slabs[3] = project_back(slab_orders(1, 3), buffer_low, buffer_other, p_own_low, p_other)
    (slabs[0],) = project_back(slab_orders(0), buffer_low, buffer_other, p_own_low, p_other)
    summed = scatter_ring(slabs, big).astype(BF)
    summed = scatter_ring([summed[k] for k in range(4)], middle).astype(BF)
    summed = summed.reshape(HALF, 4, 128).transpose(1, 0, 2)
    summed = rotate(summed, z)
    q_block = scatter_ring([summed[k] for k in range(4)], deep).astype(BF)
    p_from_other = swap_cores(p_other)

    p_chip = jnp.stack(by_core(p_own_low, p_other))
    p_pair = by_half(p_chip, swap_y_hi(p_chip))
    p_tile = rotate(jnp.stack(gather_ring(p_pair, deep)), (4 - z) % 4)
    p_tile = p_tile.transpose(1, 0, 2, 3, 4).reshape(16 * rows, HALF)
    p_tile_other = swap_cores(p_tile)

    early = [
        jnp.concatenate(
            [
                jnp.dot(part, weight, preferred_element_type=F32).astype(BF),
                jnp.dot(part, p_tile, preferred_element_type=F32).astype(BF),
            ],
            1,
        ).reshape(4, 2, 32, -1)
        for part in (tokens_own, tokens_other)
    ]
    early = jnp.stack(by_core(*early), 2)
    early = rotate(by_half(early[:, 0], early[:, 1]).transpose(1, 0, 2, 3, 4), (4 - z) % 4)
    early = early.transpose(1, 0, 2, 3, 4).reshape(4, 2, 64, -1)
    early = rotate(early, x)
    early = scatter_ring([early[k] for k in range(4)], ("x", "x")).astype(BF)
    low = row % 2 == 0
    pairs = [(i, i ^ 16) for i in range(128)]
    kept = jnp.where(low, early[0], early[1]).astype(F32)
    early = kept + lax.ppermute(jnp.where(low, early[1], early[0]), ALL, pairs).astype(F32)
    early_tokens = early[:, UNIT:].astype(BF)
    early_tokens_other = swap_cores(early_tokens)

    q_wide = q_block.astype(F32)
    q_squares = jnp.sum(q_wide * q_wide, axis=1)
    terms = three_terms(jnp.concatenate([p_squares, q_squares[None]], 0)).reshape(12, 128)
    block = jnp.concatenate([q_block, jnp.pad(terms, ((0, 4), (0, 0)))], 0)
    stack = rotate(jnp.stack(gather_ring(block, deep)), (4 - z) % 4)
    unit = stack.transpose(1, 0, 2).reshape(HALF + 16, UNIT)
    slab = jnp.stack(gather_ring(unit, middle))
    squares = jnp.sum(slab[:, HALF : HALF + 12].astype(F32).reshape(4, 3, 4, 4, 128), axis=(0, 1, 3))
    slab = slab[:, :HALF]
    q_own = gather_ring(slab, big)
    squares = sum(gather_ring(squares, big)).reshape(2, HALF)
    q_other = [swap_cores(piece) for piece in q_own]
    scale = lax.rsqrt(squares[0] + EPSILON)
    basis_scale = lax.rsqrt(scale * scale * squares[1] + EPSILON)
    scales = jnp.stack([scale, basis_scale])
    scales_other = swap_cores(scales)

    left_own = (p_own * (scale * scale)).astype(BF)
    left_other = (p_from_other.astype(F32) * (scales_other[0] * scales_other[0])).astype(BF)
    near = [(k, j) for k in (0, 1, 3) for j in (0, 1, 3)]
    across = [(2, 0), (2, 1), (2, 3), (2, 2), (0, 2), (1, 2), (3, 2)]
    new_momentum = update_momentum(
        orders(near), near, momentum, gradient, left_own, left_other, q_own, q_other
    )
    new_momentum = update_momentum(
        orders(across), across, momentum, gradient, left_own, left_other, q_own, q_other, new_momentum
    )

    basis_block = q_wide * (scale * basis_scale)[:, None]
    left_part, right_part = basis_block[:, :64], basis_block[:, 64:]
    mine = jnp.where(first, left_part, right_part).T.astype(BF)
    theirs = jnp.where(first, right_part, left_part).T.astype(BF)
    new_basis = jnp.concatenate(by_core(mine, swap_cores(theirs)), 1)

    step_scale = STEP_SIZE * math.sqrt(total_rows * width / rank)
    tile_x, tile_y = col // 4, (col % 2) * 2 + (col // 2) % 2
    far = jnp.where(first, tile_x - x, tile_y - y) % 4
    close = jnp.where(first, tile_y - y, tile_x - x) % 4

    def tile(parts, k, j, factors):
        units = [lax.dynamic_index_in_dim(part, j, 0, keepdims=False) for part in parts]
        unit = jnp.where(k == 0, units[0], jnp.where(k == 1, units[1], jnp.where(k == 2, units[2], units[3])))
        return (unit.astype(F32) * (step_scale * factors[0] * factors[0] * factors[1])[:, None]).astype(BF)

    tile_own = tile(q_own, far, close, scales)
    tile_other = tile(q_other, close, far, scales_other)
    change = jnp.dot(p_tile, tile_own, preferred_element_type=F32) + jnp.dot(
        p_tile_other, tile_other, preferred_element_type=F32
    )
    new_weight = (weight.astype(F32) - change).astype(BF)
    late = jnp.dot(early_tokens, tile_own, preferred_element_type=F32) + jnp.dot(
        early_tokens_other, tile_other, preferred_element_type=F32
    )
    logits = ((early[:, :UNIT] - late) * total_rows ** (-0.5)).astype(BF)
    return (new_momentum, new_basis, new_weight, logits)


def solution(mesh):
    in_specs = (
        P(("row", "col"), None),
        P(("row", "col"), None),
        P(("row", "col"), None),
        P("row", "col"),
        P("col", "row"),
    )
    out_specs = (P(("row", "col"), None), P(("row", "col"), None), P("row", "col"), P("row", "col"))
    return jax.shard_map(shards, mesh=mesh, in_specs=in_specs, out_specs=out_specs, check_vma=False)
```

```python
import math

import jax
import jax.numpy as jnp
from jax import lax
from jax.experimental import pallas as pl
from jax.experimental.pallas import tpu as pltpu
from jax.sharding import PartitionSpec as P

EPSILON = 1e-06
MOMENTUM_DECAY = 0.95
STEP_SIZE = 0.3
BF = jnp.bfloat16
F32 = jnp.float32
ALL = ("row", "col")
VMEM_LIMIT = 48 * 1024 * 1024
HALF = 256
TALL = HALF + 16
UNIT = 512


def device_id(x, y, z, core):
    x, y, z = x % 4, y % 4, z % 4
    return (x * 2 + y % 2) * 16 + (y // 2) * 8 + z * 2 + core


def places():
    return [(x, y, z, c) for x in range(4) for y in range(4) for z in range(4) for c in range(2)]


def moved(place, axis, shift):
    place = list(place)
    place["xyz".index(axis)] += shift
    return device_id(*place)


def shift_by(value, axes, shift):
    pairs = [(device_id(*p), moved(p, axes[p[3]], shift)) for p in places()]
    return lax.ppermute(value, ALL, pairs)


def swap_cores(value):
    return lax.ppermute(value, ALL, [(i, i ^ 1) for i in range(128)])


def gather_ring(block, axes):
    after = shift_by(block, axes, -1)
    before = shift_by(block, axes, 1)
    across = shift_by(block, axes, 2)
    return [block, after, across, before]


def scatter_ring(blocks, axes):
    from_before = shift_by(blocks[1], axes, 1)
    from_after = shift_by(blocks[3], axes, -1)
    from_across = shift_by(blocks[2], axes, 2)
    return (
        (blocks[0].astype(F32) + from_across.astype(F32))
        + (from_before.astype(F32) + from_after.astype(F32))
    )


def rotate(stack, start):
    return lax.dynamic_slice_in_dim(jnp.concatenate([stack, stack], 0), start, 4, 0)


def after(value, *done):
    return lax.optimization_barrier((value, *done))[0]


def params():
    return pltpu.CompilerParams(vmem_limit_bytes=VMEM_LIMIT)


def column_specs(rows, count):
    return [
        pl.BlockSpec((rows, UNIT), lambda i, order, u=u: (0, order[4 * i + u])) for u in range(count)
    ]


def project(order, own, other, pieces, sums=None):
    rows = own.shape[0]
    count = len(pieces)
    last = sums is not None

    def kernel(order_ref, *refs):
        own_refs, other_refs, slabs = refs[:4], refs[4:8], refs[8 : 8 + count]
        rest = refs[8 + count :]
        step = pl.program_id(0)

        def part(columns, slab):
            total = jnp.dot(columns[0][...], slab[0], preferred_element_type=F32)
            for u in range(1, 4):
                total += jnp.dot(columns[u][...], slab[u], preferred_element_type=F32)
            return total

        if last:
            mine = rest[0][...] + part(own_refs, slabs[0])
            theirs = rest[1][...] + part(other_refs, slabs[0])
            rest[2][...] = mine
            rest[3][...] = mine.astype(BF)
            rest[4][...] = theirs.astype(BF)
            squares = jnp.sum(mine * mine + theirs * theirs, axis=0, keepdims=True)
            low, high = (jnp.concatenate([squares[:, at : at + 128]] * 4, 1) for at in (0, 128))
            line = lax.broadcasted_iota(jnp.int32, (16, UNIT), 0)
            rest[5][...] = jnp.where(line == 0, low, jnp.where(line == 1, high, 0.0)).astype(BF)
            return
        for k, slab in enumerate(slabs):

            @pl.when(step == k)
            def _(slab=slab, k=k):
                mine, theirs = part(own_refs, slab), part(other_refs, slab)
                rest[0][...] = mine if k == 0 else rest[0][...] + mine
                rest[1][...] = theirs if k == 0 else rest[1][...] + theirs

    whole = pl.BlockSpec((rows, HALF), lambda i, order: (0, 0))
    slab_spec = pl.BlockSpec((4, UNIT, HALF), lambda i, order: (0, 0, 0))
    shape = lambda dtype: jax.ShapeDtypeStruct((rows, HALF), dtype)
    in_specs = column_specs(rows, 4) * 2 + [slab_spec] * count
    out_specs, out_shape = [whole, whole], [shape(F32), shape(F32)]
    if last:
        in_specs += [whole, whole]
        out_specs = [whole, whole, whole, pl.BlockSpec((16, UNIT), lambda i, order: (0, 0))]
        out_shape = [shape(F32), shape(BF), shape(BF), jax.ShapeDtypeStruct((16, UNIT), BF)]
    return pl.pallas_call(
        kernel,
        grid_spec=pltpu.PrefetchScalarGridSpec(
            num_scalar_prefetch=1, grid=(count,), in_specs=in_specs, out_specs=out_specs
        ),
        out_shape=out_shape,
        compiler_params=params(),
    )(order, *([own] * 4), *([other] * 4), *pieces, *(sums or ()))


def project_back(order, own, other, p_own, p_other, squares):
    rows = own.shape[0]
    count = order.shape[0] // 4
    contract = (((0,), (0,)), ((), ()))

    def kernel(order_ref, *refs):
        own_refs, other_refs, outs = refs[:4], refs[4:8], refs[11:]
        p_own_ref, p_other_ref, squares_ref = refs[8:11]
        step = pl.program_id(0)
        for k, out in enumerate(outs):

            @pl.when(step == k)
            def _(out=out):
                for u in range(4):
                    value = lax.dot_general(
                        p_own_ref[...], own_refs[u][...], contract, preferred_element_type=F32
                    )
                    value += lax.dot_general(
                        p_other_ref[...], other_refs[u][...], contract, preferred_element_type=F32
                    )
                    out[u, :HALF] = value.astype(BF)
                    out[u, HALF:] = squares_ref[...]

    whole = pl.BlockSpec((rows, HALF), lambda i, order: (0, 0))
    return pl.pallas_call(
        kernel,
        grid_spec=pltpu.PrefetchScalarGridSpec(
            num_scalar_prefetch=1,
            grid=(count,),
            in_specs=column_specs(rows, 4) * 2
            + [whole, whole, pl.BlockSpec((16, UNIT), lambda i, order: (0, 0))],
            out_specs=[pl.BlockSpec((4, TALL, UNIT), lambda i, order: (0, 0, 0))] * count,
        ),
        out_shape=[jax.ShapeDtypeStruct((4, TALL, UNIT), BF)] * count,
        compiler_params=params(),
    )(order, *([own] * 4), *([other] * 4), p_own, p_other, squares)


def update_momentum(order, units, momentum, gradient, left_own, left_other, q_own, q_other, previous=None):
    rows, width = momentum.shape
    count = len(units)
    own = sorted({k for k, _ in units})
    other = sorted({j for _, j in units})

    def kernel(order_ref, lo_ref, lp_ref, m_ref, g_ref, *refs):
        own_refs = dict(zip(own, refs))
        other_refs = dict(zip(other, refs[len(own) :]))
        out_ref, m_all, g_all, qo_all, qp_all, out_all, in_sems, out_sems = refs[-8:]
        loads, stores = [], []
        for n, (k, j) in enumerate(units):
            columns = pl.ds(pl.multiple_of(order_ref[n] * UNIT, UNIT), UNIT)
            pairs = (
                (m_ref.at[:, columns], m_all.at[n]),
                (g_ref.at[:, columns], g_all.at[n]),
                (own_refs[k].at[j, pl.ds(0, HALF)], qo_all.at[n]),
                (other_refs[j].at[k, pl.ds(0, HALF)], qp_all.at[n]),
            )
            loads.append(
                [pltpu.make_async_copy(a, b, in_sems.at[n, i]) for i, (a, b) in enumerate(pairs)]
            )
            stores.append(pltpu.make_async_copy(out_all.at[n], out_ref.at[:, columns], out_sems.at[n]))
        for copies in loads:
            for copy in copies:
                copy.start()
        for n in range(count):
            for copy in loads[n]:
                copy.wait()
            change = jnp.dot(lo_ref[...], qo_all[n], preferred_element_type=F32)
            change += jnp.dot(lp_ref[...], qp_all[n], preferred_element_type=F32)
            out_all[n] = (m_all[n] + g_all[n].astype(F32)) - (1.0 - MOMENTUM_DECAY) * change
            stores[n].start()
        for copy in stores:
            copy.wait()

    anywhere = pl.BlockSpec(memory_space=pl.ANY)
    operands = [order, left_own, left_other, momentum, gradient]
    in_specs = [pl.BlockSpec(memory_space=pltpu.SMEM)] + [pl.BlockSpec(memory_space=pltpu.VMEM)] * 2
    in_specs += [anywhere] * 2
    operands += [q_own[k] for k in own] + [q_other[j] for j in other]
    in_specs += [anywhere] * (len(own) + len(other))
    aliases = {}
    if previous is not None:
        aliases = {len(operands): 0}
        operands.append(previous)
        in_specs.append(anywhere)
    return pl.pallas_call(
        kernel,
        in_specs=in_specs,
        out_specs=anywhere,
        out_shape=jax.ShapeDtypeStruct((rows, width), F32),
        scratch_shapes=[
            pltpu.VMEM((count, rows, UNIT), F32),
            pltpu.VMEM((count, rows, UNIT), BF),
            pltpu.VMEM((count, HALF, UNIT), BF),
            pltpu.VMEM((count, HALF, UNIT), BF),
            pltpu.VMEM((count, rows, UNIT), F32),
            pltpu.SemaphoreType.DMA((count, 4)),
            pltpu.SemaphoreType.DMA((count,)),
        ],
        input_output_aliases=aliases,
        compiler_params=params(),
    )(*operands)


def three_terms(value):
    high = value.astype(BF)
    rest = value - high.astype(F32)
    middle = rest.astype(BF)
    return jnp.stack([high, middle, (rest - middle.astype(F32)).astype(BF)])


def shards(momentum, gradient, right_basis, weight, tokens):
    row, col = lax.axis_index("row"), lax.axis_index("col")
    x, y, z, core = row // 2, (col // 8) * 2 + row % 2, (col // 2) % 4, col % 2
    first = core == 0
    total_rows = momentum.shape[0] * 128
    rank = right_basis.shape[1]
    width = momentum.shape[1]
    rows = momentum.shape[0]
    big, middle = ("x", "y"), ("y", "x")
    deep = ("z", "z")

    def unit_at(k, j):
        ux = jnp.where(first, x + k, x + j) % 4
        uy = jnp.where(first, y + j, y + k) % 4
        return ux * 4 + (uy % 2) * 2 + uy // 2

    def orders(units):
        return jnp.stack([unit_at(k, j) for k, j in units]).astype(jnp.int32)

    def slab_orders(*slabs):
        return orders([(k, j) for k in slabs for j in range(4)])

    def halves(a):
        low, high = a[:, :HALF], a[:, HALF:]
        return jnp.where(first, low, high), jnp.where(first, high, low)

    def by_core(mine, theirs):
        return jnp.where(first, mine, theirs), jnp.where(first, theirs, mine)

    def by_half(mine, theirs):
        low = y < 2
        return jnp.stack([jnp.where(low, mine, theirs), jnp.where(low, theirs, mine)])

    def swap_y_hi(value):
        return shift_by(value, ("y", "y"), 2)

    basis_own, basis_sent = halves(right_basis)
    basis_other = swap_cores(basis_sent)
    basis_chip = jnp.concatenate(by_core(basis_own, basis_other), 0)
    stack = jnp.stack(gather_ring(basis_chip, deep))
    unit = rotate(stack, (4 - z) % 4).reshape(UNIT, HALF)
    slab = jnp.stack(gather_ring(unit, middle))
    pieces = gather_ring(slab, big)

    momentum_in, gradient_in, tokens, _ = lax.optimization_barrier((momentum, gradient, tokens, unit))
    buffer_low = (momentum_in + gradient_in.astype(F32)).astype(BF)
    buffer_other = swap_cores(buffer_low)

    tokens_pair = jnp.concatenate([tokens, swap_y_hi(tokens)], 0)
    tokens_own = jnp.concatenate(gather_ring(tokens_pair, deep), 0)
    tokens_other = swap_cores(tokens_own)

    sums = project(slab_orders(0, 1, 3), buffer_low, buffer_other, [pieces[0], pieces[1], pieces[3]])
    p_own, p_own_low, p_other, squares = project(
        slab_orders(2), buffer_low, buffer_other, [pieces[2]], sums
    )

    slabs = [None] * 4
    (slabs[2],) = project_back(slab_orders(2), buffer_low, buffer_other, p_own_low, p_other, squares)
    slabs[1], slabs[3] = project_back(slab_orders(1, 3), buffer_low, buffer_other, p_own_low, p_other, squares)
    (slabs[0],) = project_back(slab_orders(0), buffer_low, buffer_other, p_own_low, p_other, squares)
    summed = scatter_ring(slabs, big).astype(BF)
    summed = scatter_ring([summed[k] for k in range(4)], middle).astype(BF)
    summed = summed.reshape(TALL, 4, 128).transpose(1, 0, 2)
    summed = rotate(summed, z)
    summed = scatter_ring([summed[k] for k in range(4)], deep)
    q_block = summed[:HALF].astype(BF)
    scale = lax.rsqrt(summed[HALF : HALF + 2].reshape(HALF) + EPSILON)
    p_own_sent, p_other_sent, old_weight, _ = lax.optimization_barrier(
        (p_own_low, p_other, weight, slabs[0])
    )

    p_chip = jnp.stack(by_core(p_own_sent, p_other_sent))
    p_pair = by_half(p_chip, swap_y_hi(p_chip))
    p_ring = after(jnp.stack(gather_ring(p_pair, deep)), q_block)
    p_tile = rotate(p_ring, (4 - z) % 4)
    p_tile = p_tile.transpose(1, 0, 2, 3, 4).reshape(16 * rows, HALF)
    p_tile_other = swap_cores(p_tile)

    early = [
        jnp.concatenate(
            [
                jnp.dot(part, old_weight, preferred_element_type=F32).astype(BF),
                jnp.dot(part, p_tile, preferred_element_type=F32).astype(BF),
            ],
            1,
        ).reshape(4, 2, 32, -1)
        for part in (tokens_own, tokens_other)
    ]
    early = jnp.stack(by_core(*early), 2)
    early = rotate(by_half(early[:, 0], early[:, 1]).transpose(1, 0, 2, 3, 4), (4 - z) % 4)
    early = early.transpose(1, 0, 2, 3, 4).reshape(4, 2, 64, -1)
    early = rotate(early, x)
    early = scatter_ring([early[k] for k in range(4)], ("x", "x")).astype(BF)
    low = row % 2 == 0
    pairs = [(i, i ^ 16) for i in range(128)]
    kept = jnp.where(low, early[0], early[1]).astype(F32)
    early = kept + lax.ppermute(jnp.where(low, early[1], early[0]), ALL, pairs).astype(F32)
    early_tokens = early[:, UNIT:].astype(BF)
    early_tokens_other = swap_cores(early_tokens)

    q_wide = q_block.astype(F32)
    terms = three_terms(jnp.sum(q_wide * q_wide, axis=1)).reshape(6, 128)
    block = jnp.concatenate([q_block, jnp.pad(terms, ((0, 10), (0, 0)))], 0)
    stack = rotate(jnp.stack(gather_ring(block, deep)), (4 - z) % 4)
    unit = stack.transpose(1, 0, 2).reshape(TALL, UNIT)
    slab = jnp.stack(gather_ring(unit, middle))
    q_own = gather_ring(slab, big)
    q_other = [swap_cores(q_own[k]) if k != 2 else None for k in range(4)]

    squared = scale * scale
    left_own = (p_own * squared).astype(BF)
    left_other = swap_cores((p_other.astype(F32) * squared).astype(BF))
    near = [(k, j) for k in (0, 1, 3) for j in (0, 1, 3)]
    across = [(2, 0), (2, 1), (2, 3), (0, 2), (1, 2), (3, 2), (2, 2)]
    new_momentum = update_momentum(
        orders(near), near, momentum, gradient, left_own, left_other, q_own, q_other
    )
    q_other[2] = swap_cores(after(q_own[2], new_momentum))
    new_momentum = update_momentum(
        orders(across), across, momentum, gradient, left_own, left_other, q_own, q_other, new_momentum
    )

    squares = sum(
        jnp.sum(part[:, HALF : HALF + 6].astype(F32).reshape(4, 3, 2, 4, 128), axis=(0, 1, 3))
        for part in q_own
    ).reshape(HALF)
    basis_scale = lax.rsqrt(squared * squares + EPSILON)
    factor = squared * basis_scale
    factor_other = swap_cores(factor)

    basis_block = q_wide * (scale * basis_scale)[:, None]
    left_part, right_part = basis_block[:, :64], basis_block[:, 64:]
    mine = jnp.where(first, left_part, right_part).T.astype(BF)
    theirs = jnp.where(first, right_part, left_part).T.astype(BF)
    new_basis = jnp.concatenate(by_core(mine, swap_cores(theirs)), 1)

    step_scale = STEP_SIZE * math.sqrt(total_rows * width / rank)
    tile_x, tile_y = col // 4, (col % 2) * 2 + (col // 2) % 2
    far = jnp.where(first, tile_x - x, tile_y - y) % 4
    close = jnp.where(first, tile_y - y, tile_x - x) % 4

    def tile(parts, k, j, factor):
        units = [lax.dynamic_index_in_dim(part, j, 0, keepdims=False)[:HALF] for part in parts]
        unit = jnp.where(k == 0, units[0], jnp.where(k == 1, units[1], jnp.where(k == 2, units[2], units[3])))
        return (unit.astype(F32) * (step_scale * factor)[:, None]).astype(BF)

    tile_own = tile(q_own, far, close, factor)
    tile_other = tile(q_other, close, far, factor_other)
    change = jnp.dot(p_tile, tile_own, preferred_element_type=F32) + jnp.dot(
        p_tile_other, tile_other, preferred_element_type=F32
    )
    new_weight = (weight.astype(F32) - change).astype(BF)
    late = jnp.dot(early_tokens, tile_own, preferred_element_type=F32) + jnp.dot(
        early_tokens_other, tile_other, preferred_element_type=F32
    )
    logits = ((early[:, :UNIT] - late) * total_rows ** (-0.5)).astype(BF)
    return (new_momentum, new_basis, new_weight, logits)


def solution(mesh):
    in_specs = (
        P(("row", "col"), None),
        P(("row", "col"), None),
        P(("row", "col"), None),
        P("row", "col"),
        P("col", "row"),
    )
    out_specs = (P(("row", "col"), None), P(("row", "col"), None), P("row", "col"), P("row", "col"))
    return jax.shard_map(shards, mesh=mesh, in_specs=in_specs, out_specs=out_specs, check_vma=False)
```

```python
import math

import jax
import jax.numpy as jnp
from jax import lax
from jax.experimental import pallas as pl
from jax.experimental.pallas import tpu as pltpu
from jax.sharding import PartitionSpec as P

EPSILON = 1e-06
MOMENTUM_DECAY = 0.95
STEP_SIZE = 0.3
BF = jnp.bfloat16
F32 = jnp.float32
ALL = ("row", "col")
VMEM_LIMIT = 48 * 1024 * 1024
HALF = 256
TALL = HALF + 32
UNIT = 512


def device_id(x, y, z, core):
    x, y, z = x % 4, y % 4, z % 4
    return (x * 2 + y % 2) * 16 + (y // 2) * 8 + z * 2 + core


def places():
    return [(x, y, z, c) for x in range(4) for y in range(4) for z in range(4) for c in range(2)]


def moved(place, axis, shift):
    place = list(place)
    place["xyz".index(axis)] += shift
    return device_id(*place)


def shift_by(value, axes, shift):
    pairs = [(device_id(*p), moved(p, axes[p[3]], shift)) for p in places()]
    return lax.ppermute(value, ALL, pairs)


def gather_z(value):
    groups = [[y * 8 + z * 2 + c for z in range(4)] for y in range(2) for c in range(2)]
    return lax.all_gather(value, "col", axis=0, axis_index_groups=groups, tiled=True)


def exchange(value, axis, distance):
    pairs = []
    for p in places():
        other = list(p)
        other["xyz".index(axis)] ^= distance
        pairs.append((device_id(*p), device_id(*other)))
    return lax.ppermute(value, ALL, pairs)


def swap_y_lo(value):
    return exchange(value, "y", 1)


def swap_cores(value):
    return lax.ppermute(value, ALL, [(i, i ^ 1) for i in range(128)])


def gather_ring(block, axes, far_block=None):
    ahead = shift_by(block, axes, -1)
    before = shift_by(block, axes, 1)
    across = shift_by(block if far_block is None else far_block, axes, 2)
    return [block, ahead, across, before]


def scatter_ring(blocks, axes, done=None):
    from_before = shift_by(blocks[1], axes, 1)
    from_after = shift_by(blocks[3], axes, -1)
    from_across = shift_by(blocks[2], axes, 2)
    if done is not None:
        from_across = after(from_across, *done)
    return (
        (blocks[0].astype(F32) + from_across.astype(F32))
        + (from_before.astype(F32) + from_after.astype(F32))
    )


def rotate(stack, start):
    return lax.dynamic_slice_in_dim(jnp.concatenate([stack, stack], 0), start, 4, 0)


def after(value, *done):
    return lax.optimization_barrier((value, *done))[0]


def params():
    return pltpu.CompilerParams(vmem_limit_bytes=VMEM_LIMIT)


def column_specs(rows, count):
    return [
        pl.BlockSpec((rows, UNIT), lambda i, order, u=u: (0, order[4 * i + u])) for u in range(count)
    ]


def project(order, own, other, pieces, sums=None, tokens=()):
    rows = own.shape[0]
    count = len(pieces)
    last = sums is not None

    def kernel(order_ref, *refs):
        own_refs, other_refs, slabs = refs[:4], refs[4:8], refs[8 : 8 + count]
        rest = refs[8 + count :]
        step = pl.program_id(0)

        def part(columns, slab):
            total = jnp.dot(columns[0][...], slab[0], preferred_element_type=F32)
            for u in range(1, 4):
                total += jnp.dot(columns[u][...], slab[u], preferred_element_type=F32)
            return total

        if last:
            mine = rest[0][...] + part(own_refs, slabs[0])
            theirs = rest[1][...] + part(other_refs, slabs[0])
            rest[4][...] = mine
            rest[5][...] = mine.astype(BF)
            rest[6][...] = theirs.astype(BF)
            squares = jnp.sum(mine * mine + theirs * theirs, axis=0, keepdims=True)
            low, high = (jnp.concatenate([squares[:, at : at + 128]] * 4, 1) for at in (0, 128))
            line = lax.broadcasted_iota(jnp.int32, (16, UNIT), 0)
            squares = jnp.where(line == 0, low, jnp.where(line == 1, high, 0.0)).astype(BF)
            product = jnp.dot(rest[2][...], rest[5][...], preferred_element_type=F32)
            product += jnp.dot(rest[3][...], rest[6][...], preferred_element_type=F32)
            for u in range(16):
                eight = [product[at : at + 8] for at in range(32 * u, 32 * u + 32, 8)]
                eight = [jnp.concatenate([e[:, :128], e[:, 128:]], 0) for e in eight]
                rest[7][u, :16] = squares
                rest[7][u, 16:] = jnp.concatenate(eight, 1).astype(BF)
            return
        for k, slab in enumerate(slabs):

            @pl.when(step == k)
            def _(slab=slab, k=k):
                mine, theirs = part(own_refs, slab), part(other_refs, slab)
                rest[0][...] = mine if k == 0 else rest[0][...] + mine
                rest[1][...] = theirs if k == 0 else rest[1][...] + theirs

    whole = pl.BlockSpec((rows, HALF), lambda i, order: (0, 0))
    slab_spec = pl.BlockSpec((4, UNIT, HALF), lambda i, order: (0, 0, 0))
    shape = lambda dtype: jax.ShapeDtypeStruct((rows, HALF), dtype)
    in_specs = column_specs(rows, 4) * 2 + [slab_spec] * count
    out_specs, out_shape = [whole, whole], [shape(F32), shape(F32)]
    if last:
        in_specs += [whole, whole] + [pl.BlockSpec(t.shape, lambda i, order: (0, 0)) for t in tokens]
        out_specs = [whole, whole, whole, pl.BlockSpec((16, 32, UNIT), lambda i, order: (0, 0, 0))]
        out_shape = [shape(F32), shape(BF), shape(BF), jax.ShapeDtypeStruct((16, 32, UNIT), BF)]
    return pl.pallas_call(
        kernel,
        grid_spec=pltpu.PrefetchScalarGridSpec(
            num_scalar_prefetch=1, grid=(count,), in_specs=in_specs, out_specs=out_specs
        ),
        out_shape=out_shape,
        compiler_params=params(),
    )(order, *([own] * 4), *([other] * 4), *pieces, *(sums or ()), *tokens)


def project_back(order, own, other, p_own, p_other, below):
    rows = own.shape[0]
    count = order.shape[0] // 4
    contract = (((0,), (0,)), ((), ()))

    def kernel(order_ref, *refs):
        own_refs, other_refs, below_refs, outs = refs[:4], refs[4:8], refs[10:14], refs[14:]
        p_own_ref, p_other_ref = refs[8:10]
        step = pl.program_id(0)
        for k, out in enumerate(outs):

            @pl.when(step == k)
            def _(out=out):
                for u in range(4):
                    value = lax.dot_general(
                        p_own_ref[...], own_refs[u][...], contract, preferred_element_type=F32
                    )
                    value += lax.dot_general(
                        p_other_ref[...], other_refs[u][...], contract, preferred_element_type=F32
                    )
                    out[u, :HALF] = value.astype(BF)
                    out[u, HALF:] = below_refs[u][0]

    whole = pl.BlockSpec((rows, HALF), lambda i, order: (0, 0))
    return pl.pallas_call(
        kernel,
        grid_spec=pltpu.PrefetchScalarGridSpec(
            num_scalar_prefetch=1,
            grid=(count,),
            in_specs=column_specs(rows, 4) * 2
            + [whole, whole]
            + [
                pl.BlockSpec((1, 32, UNIT), lambda i, order, u=u: (order[4 * i + u], 0, 0))
                for u in range(4)
            ],
            out_specs=[pl.BlockSpec((4, TALL, UNIT), lambda i, order: (0, 0, 0))] * count,
        ),
        out_shape=[jax.ShapeDtypeStruct((4, TALL, UNIT), BF)] * count,
        compiler_params=params(),
    )(order, *([own] * 4), *([other] * 4), p_own, p_other, *([below] * 4))


def update_momentum(order, units, momentum, gradient, left_own, left_other, q_own, q_other, tile=None):
    rows, width = momentum.shape
    count = len(units)
    own = sorted({k for k, _ in units})
    other = sorted({j for _, j in units})
    chunks = 3

    def kernel(order_ref, lo_ref, lp_ref, m_ref, g_ref, *refs):
        own_refs = dict(zip(own, refs))
        other_refs = dict(zip(other, refs[len(own) :]))
        refs = refs[len(own) + len(other) :]
        if tile is not None:
            _, place_ref, f_ref, *small_refs, w_ref, po_ref, pp_ref = refs[:9]
            new_ref, logits_ref, basis_ref = refs[10:13]
            (early_ref, mine_ref, theirs_ref), refs_left = refs[-4:-1], refs[:-4]
            small_sems = refs[-1]
            w_all, po_all, pp_all, w_out, unit, scaled, lines, w_sems, unit_sems, w_out_sems = refs_left[-10:]
            out_ref, refs = refs[9], refs_left[13:-10]
        else:
            out_ref, refs = refs[0], refs[1:]
        m_all, g_all, qo_all, qp_all, out_all, in_sems, out_sems = refs
        loads, stores = [], []
        for n, (k, j) in enumerate(units):
            columns = pl.ds(pl.multiple_of(order_ref[n] * UNIT, UNIT), UNIT)
            pairs = (
                (m_ref.at[:, columns], m_all.at[n]),
                (g_ref.at[:, columns], g_all.at[n]),
                (own_refs[k].at[j, pl.ds(0, HALF)], qo_all.at[n]),
                (other_refs[j].at[k, pl.ds(0, HALF)], qp_all.at[n]),
            )
            loads.append(
                [pltpu.make_async_copy(a, b, in_sems.at[n, i]) for i, (a, b) in enumerate(pairs)]
            )
            stores.append(pltpu.make_async_copy(out_all.at[n], out_ref.at[:, columns], out_sems.at[n]))
        for copies in loads:
            for copy in copies:
                copy.start()
        if tile is not None:
            small = [
                pltpu.make_async_copy(a, b, small_sems.at[n])
                for n, (a, b) in enumerate(zip(small_refs, (early_ref, mine_ref, theirs_ref)))
            ]
            for copy in small:
                copy.start()
            wanted = []
            for side, (slabs, far, near) in enumerate(((own_refs, 0, 1), (other_refs, 1, 0))):
                wanted.append(
                    [
                        (0, pl.ds(0, HALF), unit.at[side]),
                        (2, pl.ds(HALF + 16, 16), lines.at[side, 0]),
                        (4, pl.ds(HALF + 16, 16), lines.at[side, 1]),
                    ]
                )
                for n, (at, part, target) in enumerate(wanted[side]):
                    for k in range(4):

                        @pl.when(place_ref[at + far] == k)
                        def _(slabs=slabs, side=side, n=n, at=at, near=near, part=part, target=target, k=k):
                            source = slabs[k].at[place_ref[at + near], part]
                            pltpu.make_async_copy(source, target, unit_sems.at[side, n]).start()

            chunk = w_ref.shape[0] // chunks
            parts = [pl.ds(i * chunk, chunk) for i in range(chunks)]
            w_loads = [
                [
                    pltpu.make_async_copy(a.at[part], b.at[part], w_sems.at[i, n])
                    for n, (a, b) in enumerate(((w_ref, w_all), (po_ref, po_all), (pp_ref, pp_all)))
                ]
                for i, part in enumerate(parts)
            ]
            w_stores = [
                pltpu.make_async_copy(w_out.at[part], new_ref.at[part], w_out_sems.at[i])
                for i, part in enumerate(parts)
            ]
            for copies in w_loads:
                for copy in copies:
                    copy.start()
        for n in range(count):
            for copy in loads[n]:
                copy.wait()
            change = jnp.dot(lo_ref[...], qo_all[n], preferred_element_type=F32)
            change += jnp.dot(lp_ref[...], qp_all[n], preferred_element_type=F32)
            out_all[n] = (m_all[n] + g_all[n].astype(F32)) - (1.0 - MOMENTUM_DECAY) * change
            stores[n].start()
        if tile is not None:
            for copy in small:
                copy.wait()
            core = pl.multiple_of(place_ref[6] * HALF, HALF)
            basis_ref[:, pl.ds(core, HALF)] = (mine_ref[...].astype(F32) * f_ref[2:3]).astype(BF)
            basis_ref[:, pl.ds(HALF - core, HALF)] = (
                theirs_ref[...].astype(F32) * f_ref[3:4]
            ).astype(BF)
            late = 0.0
            for side in range(2):
                for n, (_, part, target) in enumerate(wanted[side]):
                    pltpu.make_async_copy(own_refs[0].at[0, part], target, unit_sems.at[side, n]).wait()
                factor = jnp.transpose(jnp.broadcast_to(f_ref[side : side + 1], (128, HALF)))
                for at in range(0, UNIT, 128):
                    columns = slice(at, at + 128)
                    scaled[side, :, columns] = (
                        unit[side, :, columns].astype(F32) * factor
                    ).astype(BF)
                product = []
                for half in range(2):
                    block = lines[side, half].astype(F32)
                    for at in range(0, UNIT, 128):
                        eight = block[:, at : at + 128]
                        product.append(jnp.concatenate([eight[:8], eight[8:]], 1))
                product = jnp.concatenate(product, 0).astype(BF)
                late += jnp.dot(product, scaled[side], preferred_element_type=F32)
            logits_ref[...] = ((early_ref[...].astype(F32) - late) * tile[-1]).astype(BF)
            for i, part in enumerate(parts):
                for copy in w_loads[i]:
                    copy.wait()
                change = jnp.dot(po_all[part, :], scaled[0], preferred_element_type=F32)
                change += jnp.dot(pp_all[part, :], scaled[1], preferred_element_type=F32)
                w_out[part, :] = (w_all[part, :].astype(F32) - change).astype(BF)
                w_stores[i].start()
            for copy in w_stores:
                copy.wait()
        for copy in stores:
            copy.wait()

    anywhere = pl.BlockSpec(memory_space=pl.ANY)
    vmem = pl.BlockSpec(memory_space=pltpu.VMEM)
    smem = pl.BlockSpec(memory_space=pltpu.SMEM)
    operands = [order, left_own, left_other, momentum, gradient]
    in_specs = [smem, vmem, vmem, anywhere, anywhere]
    operands += [q_own[k] for k in own] + [q_other[j] for j in other]
    in_specs += [anywhere] * (len(own) + len(other))
    out_specs, out_shape = [anywhere], [jax.ShapeDtypeStruct((rows, width), F32)]
    scratch_shapes = [
        pltpu.VMEM((count, rows, UNIT), F32),
        pltpu.VMEM((count, rows, UNIT), BF),
        pltpu.VMEM((count, HALF, UNIT), BF),
        pltpu.VMEM((count, HALF, UNIT), BF),
        pltpu.VMEM((count, rows, UNIT), F32),
        pltpu.SemaphoreType.DMA((count, 4)),
        pltpu.SemaphoreType.DMA((count,)),
    ]
    aliases = {}
    if tile is not None:
        aliases = {len(operands): 0}
        operands += tile[:-1]
        in_specs += [anywhere, smem, vmem] + [anywhere] * 6
        tall, tokens = tile[6].shape[0], tile[3].shape[0]
        out_specs += [anywhere, vmem, vmem]
        out_shape += [
            jax.ShapeDtypeStruct((tall, UNIT), BF),
            jax.ShapeDtypeStruct((tokens, UNIT), BF),
            jax.ShapeDtypeStruct((tokens, UNIT), BF),
        ]
        scratch_shapes += [
            pltpu.VMEM((tall, UNIT), BF),
            pltpu.VMEM((tall, HALF), BF),
            pltpu.VMEM((tall, HALF), BF),
            pltpu.VMEM((tall, UNIT), BF),
            pltpu.VMEM((2, HALF, UNIT), BF),
            pltpu.VMEM((2, HALF, UNIT), BF),
            pltpu.VMEM((2, 2, 16, UNIT), BF),
            pltpu.SemaphoreType.DMA((chunks, 3)),
            pltpu.SemaphoreType.DMA((2, 3)),
            pltpu.SemaphoreType.DMA((chunks,)),
            pltpu.VMEM((tokens, UNIT), BF),
            pltpu.VMEM((tokens, HALF), BF),
            pltpu.VMEM((tokens, HALF), BF),
            pltpu.SemaphoreType.DMA((3,)),
        ]
    return pl.pallas_call(
        kernel,
        in_specs=in_specs,
        out_specs=out_specs,
        out_shape=out_shape,
        scratch_shapes=scratch_shapes,
        input_output_aliases=aliases,
        compiler_params=params(),
    )(*operands)


def sum_squares(slabs):
    def kernel(*refs):
        total = sum(ref[u].astype(F32) for ref in refs[:4] for u in range(4))
        total = sum(total[:, at : at + 128] for at in range(0, UNIT, 128))
        refs[4][...] = total[0:2] + total[2:4] + total[4:6]

    return pl.pallas_call(
        kernel,
        grid=(1,),
        in_specs=[pl.BlockSpec((4, 16, UNIT), lambda i: (0, HALF // 16, 0))] * 4,
        out_specs=pl.BlockSpec((2, 128), lambda i: (0, 0)),
        out_shape=jax.ShapeDtypeStruct((2, 128), F32),
        compiler_params=params(),
    )(*slabs)


def three_terms(value):
    high = value.astype(BF)
    rest = value - high.astype(F32)
    middle = rest.astype(BF)
    return jnp.stack([high, middle, (rest - middle.astype(F32)).astype(BF)])


def shards(momentum, gradient, right_basis, weight, tokens):
    row, col = lax.axis_index("row"), lax.axis_index("col")
    x, y, z, core = row // 2, (col // 8) * 2 + row % 2, (col // 2) % 4, col % 2
    first = core == 0
    total_rows = momentum.shape[0] * 128
    rank = right_basis.shape[1]
    width = momentum.shape[1]
    rows = momentum.shape[0]
    big, middle = ("x", "y"), ("y", "x")
    deep = ("z", "z")

    def unit_at(k, j):
        ux = jnp.where(first, x + k, x + j) % 4
        uy = jnp.where(first, y + j, y + k) % 4
        return ux * 4 + (uy % 2) * 2 + uy // 2

    def orders(units):
        return jnp.stack([unit_at(k, j) for k, j in units]).astype(jnp.int32)

    def slab_orders(*slabs):
        return orders([(k, j) for k in slabs for j in range(4)])

    def halves(a):
        low, high = a[:, :HALF], a[:, HALF:]
        return jnp.where(first, low, high), jnp.where(first, high, low)

    def by_core(mine, theirs):
        return jnp.where(first, mine, theirs), jnp.where(first, theirs, mine)

    def by_half(mine, theirs):
        low = y < 2
        return jnp.stack([jnp.where(low, mine, theirs), jnp.where(low, theirs, mine)])

    def swap_y_hi(value):
        return shift_by(value, ("y", "y"), 2)

    def pick(bit, values):
        return jnp.where(bit == 0, values[0], values[1]), jnp.where(bit == 0, values[1], values[0])

    basis_own, basis_sent = halves(right_basis)
    basis_other = swap_cores(basis_sent)
    basis_chip = jnp.concatenate(by_core(basis_own, basis_other), 0)
    stack = jnp.stack(gather_ring(basis_chip, deep))
    unit = rotate(stack, (4 - z) % 4).reshape(UNIT, HALF)
    tokens_near = swap_y_hi(tokens)
    unit, tokens_near = lax.optimization_barrier((unit, tokens_near))

    momentum_in, gradient_in, _ = lax.optimization_barrier((momentum, gradient, unit))
    buffer_low = (momentum_in + gradient_in.astype(F32)).astype(BF)
    slab = jnp.stack(gather_ring(unit, middle))
    slab, buffer_sent = lax.optimization_barrier((slab, buffer_low))
    pieces = gather_ring(slab, big)
    buffer_other = swap_cores(buffer_sent)

    tokens_all = lax.all_gather(
        by_half(tokens, tokens_near).reshape(64, -1), "col", axis=0,
        axis_index_groups=[[8 * k + i for i in range(8)] for k in range(2)], tiled=True,
    )
    token_parts = [
        lax.dynamic_slice_in_dim(tokens_all, rows * c, rows, 1) for c in (col, col ^ 1)
    ]

    early = jnp.dot(tokens_all, weight, preferred_element_type=F32).astype(BF)
    early = early.reshape(4, 2, 2, 32, -1).transpose(2, 0, 1, 3, 4).reshape(2, 2, 2, 64, -1)
    pieces[3], early, *token_parts = lax.optimization_barrier((pieces[3], early, *token_parts))

    def halve(value, bit, send):
        kept, sent = pick(bit, value)
        return (kept.astype(F32) + send(sent).astype(F32)).astype(BF)

    sums = project(slab_orders(0, 1, 3), buffer_low, buffer_other, [pieces[0], pieces[1], pieces[3]])
    p_own, p_own_low, p_other, below = project(
        slab_orders(2), buffer_low, buffer_other, [pieces[2]], sums, token_parts
    )

    slabs = [None] * 4
    (slabs[2],) = project_back(slab_orders(2), buffer_low, buffer_other, p_own_low, p_other, below)
    slabs[1], slabs[3] = project_back(
        slab_orders(1, 3), buffer_low, buffer_other, p_own_low, p_other, below
    )
    (slabs[0],) = project_back(slab_orders(0), buffer_low, buffer_other, p_own_low, p_other, below)
    early, p_own_sent, p_other_sent, _ = lax.optimization_barrier(
        (early, p_own_low, p_other, slabs[2])
    )
    early = halve((early[:, :, 0], early[:, :, 1]), row % 2, swap_y_lo)
    p_chip = jnp.stack(by_core(p_own_sent, p_other_sent))
    p_pair = by_half(p_chip, swap_y_hi(p_chip))
    summed = scatter_ring(slabs, big, (early, p_pair)).astype(BF)
    p_tile = gather_z(p_pair[None])
    early = halve((early[:, 0], early[:, 1]), x % 2, lambda v: exchange(after(v, summed), "x", 1))
    summed = scatter_ring([summed[k] for k in range(4)], middle, (early,)).astype(BF)
    early = halve((early[0], early[1]), x // 2, lambda v: exchange(after(v, summed), "x", 2))
    summed = summed.reshape(TALL, 4, 128).transpose(1, 0, 2)
    summed = rotate(summed, z)
    summed = scatter_ring([summed[k] for k in range(4)], deep)
    q_block = summed[:HALF].astype(BF)
    scale = lax.rsqrt(summed[HALF : HALF + 2].reshape(HALF) + EPSILON)

    p_tile = after(p_tile, q_block).transpose(1, 0, 2, 3, 4).reshape(16 * rows, HALF)
    p_tile_other = swap_cores(p_tile)

    left_part, right_part = q_block[:, :64].T, q_block[:, 64:].T
    mine = jnp.where(first, left_part, right_part)
    theirs = swap_cores(jnp.where(first, right_part, left_part))
    squared = scale * scale
    left_own = (p_own * squared).astype(BF)
    left_other = swap_cores((p_other.astype(F32) * squared).astype(BF))

    q_wide = q_block.astype(F32)
    terms = three_terms(jnp.sum(q_wide * q_wide, axis=1)).reshape(6, 128)
    block = jnp.concatenate([q_block, jnp.pad(terms, ((0, 10), (0, 0))), summed[HALF + 16 :].astype(BF)], 0)
    stack = rotate(jnp.stack(gather_ring(block, deep)), (4 - z) % 4)
    unit = stack.transpose(1, 0, 2).reshape(TALL, UNIT)
    slab = jnp.stack(gather_ring(unit, middle))
    slab, mine, theirs, left_own, left_other, early = lax.optimization_barrier(
        (slab, mine, theirs, left_own, left_other, early)
    )
    q_own = gather_ring(slab, big)
    q_other = [swap_cores(q_own[k]) if k != 2 else None for k in range(4)]

    near = [(k, j) for k in (0, 1, 3) for j in (0, 1, 3)]
    across = [(2, 0), (2, 1), (2, 3), (0, 2), (1, 2), (3, 2), (2, 2)]
    (new_momentum,) = update_momentum(
        orders(near), near, momentum, gradient, left_own, left_other, q_own, q_other
    )
    q_own[2] = after(q_own[2], new_momentum)
    q_other[2] = swap_cores(q_own[2])
    squares = sum_squares(q_own).reshape(HALF)
    basis_scale = lax.rsqrt(squared * squares + EPSILON)
    factors = jnp.stack([squared * basis_scale, scale * basis_scale])
    factors_other = swap_cores(factors)

    def place_of(unit):
        dx, dy = (unit // 4 - x) % 4, ((unit % 2) * 2 + (unit // 2) % 2 - y) % 4
        return [jnp.where(first, dx, dy), jnp.where(first, dy, dx)]

    block = (row % 4) * 4 + row // 4
    place = place_of(col) + place_of(block) + place_of(block + 2) + [core]
    step_scale = STEP_SIZE * math.sqrt(total_rows * width / rank)
    factors, factors_other = factors * jnp.array([[step_scale], [1.0]], F32), factors_other * jnp.array(
        [[step_scale], [1.0]], F32
    )
    tile = [
        new_momentum,
        jnp.stack(place).astype(jnp.int32),
        jnp.stack([factors[0], factors_other[0], factors[1], factors_other[1]]),
        early,
        mine,
        theirs,
        weight,
        p_tile,
        p_tile_other,
        total_rows ** (-0.5),
    ]
    new_momentum, new_weight, logits, new_basis = update_momentum(
        orders(across), across, momentum, gradient, left_own, left_other, q_own, q_other, tile
    )
    return (new_momentum, new_basis, new_weight, logits)


def solution(mesh):
    in_specs = (
        P(("row", "col"), None),
        P(("row", "col"), None),
        P(("row", "col"), None),
        P("row", "col"),
        P("col", "row"),
    )
    out_specs = (P(("row", "col"), None), P(("row", "col"), None), P("row", "col"), P("row", "col"))
    return jax.shard_map(shards, mesh=mesh, in_specs=in_specs, out_specs=out_specs, check_vma=False)
```

```python
import math

import jax
import jax.numpy as jnp
from jax import lax
from jax.experimental import pallas as pl
from jax.experimental.pallas import tpu as pltpu
from jax.sharding import PartitionSpec as P

EPSILON = 1e-06
MOMENTUM_DECAY = 0.95
STEP_SIZE = 0.3
BF = jnp.bfloat16
F32 = jnp.float32
ALL = ("row", "col")
VMEM_LIMIT = 48 * 1024 * 1024
HALF = 256
TALL = HALF + 32
UNIT = 512


def device_id(x, y, z, core):
    x, y, z = x % 4, y % 4, z % 4
    return (x * 2 + y % 2) * 16 + (y // 2) * 8 + z * 2 + core


def places():
    return [(x, y, z, c) for x in range(4) for y in range(4) for z in range(4) for c in range(2)]


def moved(place, axis, shift):
    place = list(place)
    place["xyz".index(axis)] += shift
    return device_id(*place)


def shift_by(value, axes, shift):
    pairs = [(device_id(*p), moved(p, axes[p[3]], shift)) for p in places()]
    return lax.ppermute(value, ALL, pairs)


def gather_z(value):
    groups = [[y * 8 + z * 2 + c for z in range(4)] for y in range(2) for c in range(2)]
    return lax.all_gather(value, "col", axis=0, axis_index_groups=groups, tiled=True)


def exchange(value, axis, distance):
    pairs = []
    for p in places():
        other = list(p)
        other["xyz".index(axis)] ^= distance
        pairs.append((device_id(*p), device_id(*other)))
    return lax.ppermute(value, ALL, pairs)


def swap_y_lo(value):
    return exchange(value, "y", 1)


def swap_cores(value):
    return lax.ppermute(value, ALL, [(i, i ^ 1) for i in range(128)])


def gather_ring(block, axes, far_block=None):
    ahead = shift_by(block, axes, -1)
    before = shift_by(block, axes, 1)
    across = shift_by(block if far_block is None else far_block, axes, 2)
    return [block, ahead, across, before]


def scatter_ring(blocks, axes, done=None):
    from_before = shift_by(blocks[1], axes, 1)
    from_after = shift_by(blocks[3], axes, -1)
    from_across = shift_by(blocks[2], axes, 2)
    if done is not None:
        from_across = after(from_across, *done)
    return (
        (blocks[0].astype(F32) + from_across.astype(F32))
        + (from_before.astype(F32) + from_after.astype(F32))
    )


def rotate(stack, start):
    return lax.dynamic_slice_in_dim(jnp.concatenate([stack, stack], 0), start, 4, 0)


def in_hbm(value):
    return pltpu.with_memory_space_constraint(value, pltpu.HBM)


def after(value, *done):
    return lax.optimization_barrier((value, *done))[0]


def params():
    return pltpu.CompilerParams(vmem_limit_bytes=VMEM_LIMIT)


def column_specs(rows, count):
    return [
        pl.BlockSpec((rows, UNIT), lambda i, order, u=u: (0, order[4 * i + u])) for u in range(count)
    ]


def project(order, own, other, pieces, sums=None, tokens=()):
    rows = own.shape[0]
    count = len(pieces)
    last = sums is not None

    def kernel(order_ref, *refs):
        own_refs, other_refs, slabs = refs[:4], refs[4:8], refs[8 : 8 + count]
        rest = refs[8 + count :]
        step = pl.program_id(0)

        def part(columns, slab):
            total = jnp.dot(columns[0][...], slab[0], preferred_element_type=F32)
            for u in range(1, 4):
                total += jnp.dot(columns[u][...], slab[u], preferred_element_type=F32)
            return total

        if last:
            mine = rest[0][...] + part(own_refs, slabs[0])
            theirs = rest[1][...] + part(other_refs, slabs[0])
            rest[4][...] = mine
            rest[5][...] = mine.astype(BF)
            rest[6][...] = theirs.astype(BF)
            squares = jnp.sum(mine * mine + theirs * theirs, axis=0, keepdims=True)
            low, high = (jnp.concatenate([squares[:, at : at + 128]] * 4, 1) for at in (0, 128))
            line = lax.broadcasted_iota(jnp.int32, (16, UNIT), 0)
            squares = jnp.where(line == 0, low, jnp.where(line == 1, high, 0.0)).astype(BF)
            product = jnp.dot(rest[2][...], rest[5][...], preferred_element_type=F32)
            product += jnp.dot(rest[3][...], rest[6][...], preferred_element_type=F32)
            for u in range(16):
                eight = [product[at : at + 8] for at in range(32 * u, 32 * u + 32, 8)]
                eight = [jnp.concatenate([e[:, :128], e[:, 128:]], 0) for e in eight]
                rest[7][u, :16] = squares
                rest[7][u, 16:] = jnp.concatenate(eight, 1).astype(BF)
            return
        for k, slab in enumerate(slabs):

            @pl.when(step == k)
            def _(slab=slab, k=k):
                mine, theirs = part(own_refs, slab), part(other_refs, slab)
                rest[0][...] = mine if k == 0 else rest[0][...] + mine
                rest[1][...] = theirs if k == 0 else rest[1][...] + theirs

    whole = pl.BlockSpec((rows, HALF), lambda i, order: (0, 0))
    slab_spec = pl.BlockSpec((4, UNIT, HALF), lambda i, order: (0, 0, 0))
    shape = lambda dtype: jax.ShapeDtypeStruct((rows, HALF), dtype)
    in_specs = column_specs(rows, 4) * 2 + [slab_spec] * count
    out_specs, out_shape = [whole, whole], [shape(F32), shape(F32)]
    if last:
        in_specs += [whole, whole] + [pl.BlockSpec(t.shape, lambda i, order: (0, 0)) for t in tokens]
        out_specs = [whole, whole, whole, pl.BlockSpec((16, 32, UNIT), lambda i, order: (0, 0, 0))]
        out_shape = [shape(F32), shape(BF), shape(BF), jax.ShapeDtypeStruct((16, 32, UNIT), BF)]
    return pl.pallas_call(
        kernel,
        grid_spec=pltpu.PrefetchScalarGridSpec(
            num_scalar_prefetch=1, grid=(count,), in_specs=in_specs, out_specs=out_specs
        ),
        out_shape=out_shape,
        compiler_params=params(),
    )(order, *([own] * 4), *([other] * 4), *pieces, *(sums or ()), *tokens)


def project_back(order, own, other, p_own, p_other, below):
    rows = own.shape[0]
    count = order.shape[0] // 4
    contract = (((0,), (0,)), ((), ()))

    def kernel(order_ref, *refs):
        own_refs, other_refs, below_refs, outs = refs[:4], refs[4:8], refs[10:14], refs[14:]
        p_own_ref, p_other_ref = refs[8:10]
        step = pl.program_id(0)
        for k, out in enumerate(outs):

            @pl.when(step == k)
            def _(out=out):
                for u in range(4):
                    value = lax.dot_general(
                        p_own_ref[...], own_refs[u][...], contract, preferred_element_type=F32
                    )
                    value += lax.dot_general(
                        p_other_ref[...], other_refs[u][...], contract, preferred_element_type=F32
                    )
                    out[u, :HALF] = value.astype(BF)
                    out[u, HALF:] = below_refs[u][0]

    whole = pl.BlockSpec((rows, HALF), lambda i, order: (0, 0))
    return pl.pallas_call(
        kernel,
        grid_spec=pltpu.PrefetchScalarGridSpec(
            num_scalar_prefetch=1,
            grid=(count,),
            in_specs=column_specs(rows, 4) * 2
            + [whole, whole]
            + [
                pl.BlockSpec((1, 32, UNIT), lambda i, order, u=u: (order[4 * i + u], 0, 0))
                for u in range(4)
            ],
            out_specs=[pl.BlockSpec((4, TALL, UNIT), lambda i, order: (0, 0, 0))] * count,
        ),
        out_shape=[jax.ShapeDtypeStruct((4, TALL, UNIT), BF)] * count,
        compiler_params=params(),
    )(order, *([own] * 4), *([other] * 4), p_own, p_other, *([below] * 4))


def update_momentum(order, units, momentum, gradient, left_own, left_other, q_own, q_other, tile=None):
    rows, width = momentum.shape
    count = len(units)
    chunks = 3
    parts_of = []
    for side, slabs in enumerate((q_own, q_other)):
        for k in sorted({unit[side] for unit in units}):
            at = 0
            for part in slabs[k]:
                parts_of.append((side, k, at, part))
                at += part.shape[0]

    def find(refs, side, k, j):
        for ref, (s, slab, at, part) in zip(refs, parts_of):
            if s == side and slab == k and at <= j < at + part.shape[0]:
                return ref.at[j - at, pl.ds(0, HALF)]

    def kernel(order_ref, lo_ref, lp_ref, m_ref, g_ref, *refs):
        *refs, left_all, left_sems = refs
        slab_refs, refs = refs[: len(parts_of)], refs[len(parts_of) :]
        if tile is not None:
            _, place_ref, f_ref, *small_refs, w_ref, po_ref, pp_ref = refs[:9]
            new_ref, logits_ref, basis_ref = refs[10:13]
            (early_ref, mine_ref, theirs_ref), refs_left = refs[-4:-1], refs[:-4]
            small_sems = refs[-1]
            w_all, p_all, w_out, unit, scaled, lines, w_sems, unit_sems, w_out_sems = refs_left[-9:]
            out_ref, refs = refs[9], refs_left[13:-9]
        else:
            out_ref, refs = refs[0], refs[1:]
        m_all, g_all, q_all, out_all, in_sems, out_sems = refs
        lefts = [
            pltpu.make_async_copy(a, left_all.at[:, pl.ds(n * HALF, HALF)], left_sems.at[n])
            for n, a in enumerate((lo_ref, lp_ref))
        ]
        for copy in lefts:
            copy.start()
        loads, stores = [], []
        for n, (k, j) in enumerate(units):
            columns = pl.ds(pl.multiple_of(order_ref[n] * UNIT, UNIT), UNIT)
            pairs = (
                (m_ref.at[:, columns], m_all.at[n]),
                (g_ref.at[:, columns], g_all.at[n]),
                (find(slab_refs, 0, k, j), q_all.at[n, pl.ds(0, HALF)]),
                (find(slab_refs, 1, j, k), q_all.at[n, pl.ds(HALF, HALF)]),
            )
            loads.append(
                [pltpu.make_async_copy(a, b, in_sems.at[n, i]) for i, (a, b) in enumerate(pairs)]
            )
            stores.append(pltpu.make_async_copy(out_all.at[n], out_ref.at[:, columns], out_sems.at[n]))
        for copies in loads:
            for copy in copies:
                copy.start()
        if tile is not None:
            small = [
                pltpu.make_async_copy(a, b, small_sems.at[n])
                for n, (a, b) in enumerate(zip(small_refs, (early_ref, mine_ref, theirs_ref)))
            ]
            for copy in small:
                copy.start()
            wanted = [
                [
                    (0, pl.ds(0, HALF), unit.at[side]),
                    (2, pl.ds(HALF + 16, 16), lines.at[side, 0]),
                    (4, pl.ds(HALF + 16, 16), lines.at[side, 1]),
                ]
                for side in range(2)
            ]
            for ref, (side, k, start, values) in zip(slab_refs, parts_of):
                for n, (at, part, target) in enumerate(wanted[side]):
                    near = place_ref[at + 1 - side]
                    here = (place_ref[at + side] == k) & (near >= start)

                    @pl.when(here & (near < start + values.shape[0]))
                    def _(ref=ref, side=side, start=start, n=n, part=part, target=target, near=near):
                        source = ref.at[near - start, part]
                        pltpu.make_async_copy(source, target, unit_sems.at[side, n]).start()

            chunk = w_ref.shape[0] // chunks
            parts = [pl.ds(i * chunk, chunk) for i in range(chunks)]
            targets = (
                (w_ref, w_all),
                (po_ref, p_all.at[:, pl.ds(0, HALF)]),
                (pp_ref, p_all.at[:, pl.ds(HALF, HALF)]),
            )
            w_loads = [
                [
                    pltpu.make_async_copy(a.at[part], b.at[part], w_sems.at[i, n])
                    for n, (a, b) in enumerate(targets)
                ]
                for i, part in enumerate(parts)
            ]
            w_stores = [
                pltpu.make_async_copy(w_out.at[part], new_ref.at[part], w_out_sems.at[i])
                for i, part in enumerate(parts)
            ]
            for copies in w_loads:
                for copy in copies:
                    copy.start()
        for copy in lefts:
            copy.wait()
        left = left_all[...]
        for n in range(count):
            for copy in loads[n]:
                copy.wait()
            change = jnp.dot(left, q_all[n], preferred_element_type=F32)
            out_all[n] = (m_all[n] + g_all[n].astype(F32)) - (1.0 - MOMENTUM_DECAY) * change
            stores[n].start()
        if tile is not None:
            for copy in small:
                copy.wait()
            core = pl.multiple_of(place_ref[6] * HALF, HALF)
            basis_ref[:, pl.ds(core, HALF)] = (mine_ref[...].astype(F32) * f_ref[2:3]).astype(BF)
            basis_ref[:, pl.ds(HALF - core, HALF)] = (
                theirs_ref[...].astype(F32) * f_ref[3:4]
            ).astype(BF)
            late = 0.0
            for side in range(2):
                for n, (_, part, target) in enumerate(wanted[side]):
                    pltpu.make_async_copy(slab_refs[0].at[0, part], target, unit_sems.at[side, n]).wait()
                factor = jnp.transpose(jnp.broadcast_to(f_ref[side : side + 1], (128, HALF)))
                for at in range(0, UNIT, 128):
                    columns = slice(at, at + 128)
                    scaled[side * HALF : side * HALF + HALF, columns] = (
                        unit[side, :, columns].astype(F32) * factor
                    ).astype(BF)
                product = []
                for half in range(2):
                    block = lines[side, half].astype(F32)
                    for at in range(0, UNIT, 128):
                        eight = block[:, at : at + 128]
                        product.append(jnp.concatenate([eight[:8], eight[8:]], 1))
                product = jnp.concatenate(product, 0).astype(BF)
                late += jnp.dot(product, scaled[side * HALF : side * HALF + HALF], preferred_element_type=F32)
            logits_ref[...] = ((early_ref[...].astype(F32) - late) * tile[-1]).astype(BF)
            for i, part in enumerate(parts):
                for copy in w_loads[i]:
                    copy.wait()
                change = jnp.dot(p_all[part, :], scaled[...], preferred_element_type=F32)
                w_out[part, :] = (w_all[part, :].astype(F32) - change).astype(BF)
                w_stores[i].start()
            for copy in w_stores:
                copy.wait()
        for copy in stores:
            copy.wait()

    anywhere = pl.BlockSpec(memory_space=pl.ANY)
    vmem = pl.BlockSpec(memory_space=pltpu.VMEM)
    smem = pl.BlockSpec(memory_space=pltpu.SMEM)
    operands = [order, *map(in_hbm, (left_own, left_other)), momentum, gradient]
    in_specs = [smem, anywhere, anywhere, anywhere, anywhere]
    operands += [part for *_, part in parts_of]
    in_specs += [anywhere] * len(parts_of)
    out_specs, out_shape = [anywhere], [jax.ShapeDtypeStruct((rows, width), F32)]
    scratch_shapes = [
        pltpu.VMEM((count, rows, UNIT), F32),
        pltpu.VMEM((count, rows, UNIT), BF),
        pltpu.VMEM((count, 2 * HALF, UNIT), BF),
        pltpu.VMEM((count, rows, UNIT), F32),
        pltpu.SemaphoreType.DMA((count, 4)),
        pltpu.SemaphoreType.DMA((count,)),
    ]
    aliases = {}
    if tile is not None:
        aliases = {len(operands): 0}
        operands += [*tile[:3], *map(in_hbm, tile[3:6]), *tile[6:-1]]
        in_specs += [anywhere, smem, vmem] + [anywhere] * 6
        tall, tokens = tile[6].shape[0], tile[3].shape[0]
        out_specs += [anywhere, vmem, vmem]
        out_shape += [
            jax.ShapeDtypeStruct((tall, UNIT), BF),
            jax.ShapeDtypeStruct((tokens, UNIT), BF),
            jax.ShapeDtypeStruct((tokens, UNIT), BF),
        ]
        scratch_shapes += [
            pltpu.VMEM((tall, UNIT), BF),
            pltpu.VMEM((tall, 2 * HALF), BF),
            pltpu.VMEM((tall, UNIT), BF),
            pltpu.VMEM((2, HALF, UNIT), BF),
            pltpu.VMEM((2 * HALF, UNIT), BF),
            pltpu.VMEM((2, 2, 16, UNIT), BF),
            pltpu.SemaphoreType.DMA((chunks, 3)),
            pltpu.SemaphoreType.DMA((2, 3)),
            pltpu.SemaphoreType.DMA((chunks,)),
            pltpu.VMEM((tokens, UNIT), BF),
            pltpu.VMEM((tokens, HALF), BF),
            pltpu.VMEM((tokens, HALF), BF),
            pltpu.SemaphoreType.DMA((3,)),
        ]
    scratch_shapes += [pltpu.VMEM((rows, 2 * HALF), BF), pltpu.SemaphoreType.DMA((2,))]
    return pl.pallas_call(
        kernel,
        in_specs=in_specs,
        out_specs=out_specs,
        out_shape=out_shape,
        scratch_shapes=scratch_shapes,
        input_output_aliases=aliases,
        compiler_params=params(),
    )(*operands)


def sum_squares(parts):
    def kernel(*refs):
        total = sum(ref[u].astype(F32) for ref in refs[:-1] for u in range(ref.shape[0]))
        total = sum(total[:, at : at + 128] for at in range(0, UNIT, 128))
        refs[-1][...] = total[0:2] + total[2:4] + total[4:6]

    return pl.pallas_call(
        kernel,
        grid=(1,),
        in_specs=[pl.BlockSpec((p.shape[0], 16, UNIT), lambda i: (0, HALF // 16, 0)) for p in parts],
        out_specs=pl.BlockSpec((2, 128), lambda i: (0, 0)),
        out_shape=jax.ShapeDtypeStruct((2, 128), F32),
        compiler_params=params(),
    )(*parts)


def three_terms(value):
    high = value.astype(BF)
    rest = value - high.astype(F32)
    middle = rest.astype(BF)
    return jnp.stack([high, middle, (rest - middle.astype(F32)).astype(BF)])


def shards(momentum, gradient, right_basis, weight, tokens):
    row, col = lax.axis_index("row"), lax.axis_index("col")
    x, y, z, core = row // 2, (col // 8) * 2 + row % 2, (col // 2) % 4, col % 2
    first = core == 0
    total_rows = momentum.shape[0] * 128
    rank = right_basis.shape[1]
    width = momentum.shape[1]
    rows = momentum.shape[0]
    big, middle = ("x", "y"), ("y", "x")
    deep = ("z", "z")

    def unit_at(k, j):
        ux = jnp.where(first, x + k, x + j) % 4
        uy = jnp.where(first, y + j, y + k) % 4
        return ux * 4 + (uy % 2) * 2 + uy // 2

    def orders(units):
        return jnp.stack([unit_at(k, j) for k, j in units]).astype(jnp.int32)

    def slab_orders(*slabs):
        return orders([(k, j) for k in slabs for j in range(4)])

    def halves(a):
        low, high = a[:, :HALF], a[:, HALF:]
        return jnp.where(first, low, high), jnp.where(first, high, low)

    def by_core(mine, theirs):
        return jnp.where(first, mine, theirs), jnp.where(first, theirs, mine)

    def by_half(mine, theirs):
        low = y < 2
        return jnp.stack([jnp.where(low, mine, theirs), jnp.where(low, theirs, mine)])

    def swap_y_hi(value):
        return shift_by(value, ("y", "y"), 2)

    def pick(bit, values):
        return jnp.where(bit == 0, values[0], values[1]), jnp.where(bit == 0, values[1], values[0])

    basis_own, basis_sent = halves(right_basis)
    basis_other = swap_cores(basis_sent)
    basis_chip = jnp.concatenate(by_core(basis_own, basis_other), 0)
    stack = jnp.stack(gather_ring(basis_chip, deep))
    unit = rotate(stack, (4 - z) % 4).reshape(UNIT, HALF)
    tokens_near = swap_y_hi(tokens)
    unit, tokens_near = lax.optimization_barrier((unit, tokens_near))

    momentum_in, gradient_in, _ = lax.optimization_barrier((momentum, gradient, unit))
    buffer_low = (momentum_in + gradient_in.astype(F32)).astype(BF)
    slab = jnp.stack(gather_ring(unit, middle))
    slab, buffer_sent = lax.optimization_barrier((slab, buffer_low))
    pieces = gather_ring(slab, big)
    buffer_other = swap_cores(buffer_sent)

    tokens_all = lax.all_gather(
        by_half(tokens, tokens_near).reshape(64, -1), "col", axis=0,
        axis_index_groups=[[8 * k + i for i in range(8)] for k in range(2)], tiled=True,
    )
    token_parts = [
        lax.dynamic_slice_in_dim(tokens_all, rows * c, rows, 1) for c in (col, col ^ 1)
    ]

    early = jnp.dot(tokens_all, weight, preferred_element_type=F32).astype(BF)
    early = early.reshape(4, 2, 2, 32, -1).transpose(2, 0, 1, 3, 4).reshape(2, 2, 2, 64, -1)
    pieces[3], early, *token_parts = lax.optimization_barrier((pieces[3], early, *token_parts))

    def halve(value, bit, send):
        kept, sent = pick(bit, value)
        return (kept.astype(F32) + send(sent).astype(F32)).astype(BF)

    sums = project(slab_orders(0, 1, 3), buffer_low, buffer_other, [pieces[0], pieces[1], pieces[3]])
    p_own, p_own_low, p_other, below = project(
        slab_orders(2), buffer_low, buffer_other, [pieces[2]], sums, token_parts
    )

    p_chip = jnp.stack(by_core(p_own_low, p_other))
    p_far = swap_y_hi(p_chip)
    p_pair = by_half(p_chip, p_far)

    slabs = [None] * 4
    (slabs[2],) = project_back(slab_orders(2), buffer_low, buffer_other, p_own_low, p_other, below)
    slabs[1], slabs[3] = project_back(
        after(slab_orders(1, 3), slabs[2]), buffer_low, buffer_other, p_own_low, p_other, below
    )
    (slabs[0],) = project_back(after(slab_orders(0), slabs[1]), buffer_low, buffer_other, p_own_low, p_other, below)
    summed = scatter_ring(slabs, big, (p_pair,)).astype(BF)
    p_tile = gather_z(p_pair[None])
    early = halve((early[:, :, 0], early[:, :, 1]), row % 2, lambda v: swap_y_lo(after(v, summed)))
    summed = scatter_ring([summed[k] for k in range(4)], middle, (early,)).astype(BF)
    early = halve((early[:, 0], early[:, 1]), x % 2, lambda v: exchange(after(v, summed), "x", 1))
    summed = summed.reshape(TALL, 4, 128).transpose(1, 0, 2)
    summed = rotate(summed, z)
    summed = scatter_ring([summed[k] for k in range(4)], deep, (early,))
    early = halve((early[0], early[1]), x // 2, lambda v: exchange(after(v, summed), "x", 2))
    q_block = summed[:HALF].astype(BF)
    scale = lax.rsqrt(summed[HALF : HALF + 2].reshape(HALF) + EPSILON)

    p_tile = after(p_tile, q_block).transpose(1, 0, 2, 3, 4).reshape(16 * rows, HALF)

    left_part, right_part = q_block[:, :64].T, q_block[:, 64:].T
    mine = jnp.where(first, left_part, right_part)
    theirs = swap_cores(jnp.where(first, right_part, left_part))
    squared = scale * scale
    left_own = (p_own * squared).astype(BF)
    left_other = swap_cores((p_other.astype(F32) * squared).astype(BF))

    q_wide = q_block.astype(F32)
    terms = three_terms(jnp.sum(q_wide * q_wide, axis=1)).reshape(6, 128)
    block = jnp.concatenate([q_block, jnp.pad(terms, ((0, 10), (0, 0))), summed[HALF + 16 :].astype(BF)], 0)
    stack = rotate(jnp.stack(gather_ring(block, deep)), (4 - z) % 4)
    unit = stack.transpose(1, 0, 2).reshape(TALL, UNIT)
    unit, mine, theirs, left_own, left_other, early = lax.optimization_barrier(
        (unit, mine, theirs, left_own, left_other, early)
    )
    slab = jnp.stack(gather_ring(unit, middle))
    q_ahead, q_before = shift_by(slab, big, -1), shift_by(slab, big, 1)
    q_ahead, p_tile = lax.optimization_barrier((q_ahead, p_tile))
    q_across = [shift_by(q_ahead[:2], big, -1), shift_by(q_before[2:], big, 1)]
    p_tile_other = swap_cores(p_tile)
    q_own = [[slab], [q_ahead], q_across, [q_before]]
    q_other = [[swap_cores(part) for part in q_own[k]] if k != 2 else None for k in range(4)]

    near = [(k, j) for k in (0, 1, 3) for j in (0, 1, 3)]
    across = [(2, 0), (2, 1), (2, 3), (0, 2), (1, 2), (3, 2), (2, 2)]
    (new_momentum,) = update_momentum(
        orders(near), near, momentum, gradient, left_own, left_other, q_own, q_other
    )
    *q_own[2], _ = lax.optimization_barrier((*q_own[2], new_momentum))
    q_other[2] = [swap_cores(part) for part in q_own[2]]
    squares = sum_squares([part for parts in q_own for part in parts]).reshape(HALF)
    basis_scale = lax.rsqrt(squared * squares + EPSILON)
    factors = jnp.stack([squared * basis_scale, scale * basis_scale])
    factors_other = swap_cores(factors)

    def place_of(unit):
        dx, dy = (unit // 4 - x) % 4, ((unit % 2) * 2 + (unit // 2) % 2 - y) % 4
        return [jnp.where(first, dx, dy), jnp.where(first, dy, dx)]

    block = (row % 4) * 4 + row // 4
    place = place_of(col) + place_of(block) + place_of(block + 2) + [core]
    step_scale = STEP_SIZE * math.sqrt(total_rows * width / rank)
    factors, factors_other = factors * jnp.array([[step_scale], [1.0]], F32), factors_other * jnp.array(
        [[step_scale], [1.0]], F32
    )
    tile = [
        new_momentum,
        jnp.stack(place).astype(jnp.int32),
        jnp.stack([factors[0], factors_other[0], factors[1], factors_other[1]]),
        early,
        mine,
        theirs,
        weight,
        p_tile,
        p_tile_other,
        total_rows ** (-0.5),
    ]
    new_momentum, new_weight, logits, new_basis = update_momentum(
        orders(across), across, momentum, gradient, left_own, left_other, q_own, q_other, tile
    )
    return (new_momentum, new_basis, new_weight, logits)


def solution(mesh):
    in_specs = (
        P(("row", "col"), None),
        P(("row", "col"), None),
        P(("row", "col"), None),
        P("row", "col"),
        P("col", "row"),
    )
    out_specs = (P(("row", "col"), None), P(("row", "col"), None), P("row", "col"), P("row", "col"))
    return jax.shard_map(shards, mesh=mesh, in_specs=in_specs, out_specs=out_specs, check_vma=False)
```

```python
import math

import jax
import jax.numpy as jnp
from jax import lax
from jax.experimental import pallas as pl
from jax.experimental.pallas import tpu as pltpu
from jax.sharding import PartitionSpec as P

EPSILON = 1e-06
MOMENTUM_DECAY = 0.95
STEP_SIZE = 0.3
BF = jnp.bfloat16
F32 = jnp.float32
ALL = ("row", "col")
VMEM_LIMIT = 28 * 1024 * 1024
HALF = 256
TALL = HALF + 32
UNIT = 512


def device_id(x, y, z, core):
    x, y, z = x % 4, y % 4, z % 4
    return (x * 2 + y % 2) * 16 + (y // 2) * 8 + z * 2 + core


def places():
    return [(x, y, z, c) for x in range(4) for y in range(4) for z in range(4) for c in range(2)]


def moved(place, axis, shift):
    place = list(place)
    place["xyz".index(axis)] += shift
    return device_id(*place)


def shift_by(value, axes, shift):
    pairs = [(device_id(*p), moved(p, axes[p[3]], shift)) for p in places()]
    return lax.ppermute(value, ALL, pairs)


def gather_z(value):
    groups = [[y * 8 + z * 2 + c for z in range(4)] for y in range(2) for c in range(2)]
    return lax.all_gather(value, "col", axis=0, axis_index_groups=groups, tiled=True)


def exchange(value, axis, distance):
    pairs = []
    for p in places():
        other = list(p)
        other["xyz".index(axis)] ^= distance
        pairs.append((device_id(*p), device_id(*other)))
    return lax.ppermute(value, ALL, pairs)


def swap_y_lo(value):
    return exchange(value, "y", 1)


def swap_cores(value):
    return lax.ppermute(value, ALL, [(i, i ^ 1) for i in range(128)])


def gather_ring(block, axes, far_block=None):
    ahead = shift_by(block, axes, -1)
    before = shift_by(block, axes, 1)
    across = shift_by(block if far_block is None else far_block, axes, 2)
    return [block, ahead, across, before]


def scatter_ring(blocks, axes, done=None):
    from_before = shift_by(blocks[1], axes, 1)
    from_after = shift_by(blocks[3], axes, -1)
    from_across = shift_by(blocks[2], axes, 2)
    if done is not None:
        from_across = after(from_across, *done)
    return (
        (blocks[0].astype(F32) + from_across.astype(F32))
        + (from_before.astype(F32) + from_after.astype(F32))
    )


def rotate(stack, start):
    return lax.dynamic_slice_in_dim(jnp.concatenate([stack, stack], 0), start, 4, 0)


def in_hbm(value):
    return pltpu.with_memory_space_constraint(value, pltpu.HBM)


def after(value, *done):
    return lax.optimization_barrier((value, *done))[0]


def params():
    return pltpu.CompilerParams(vmem_limit_bytes=VMEM_LIMIT)


def column_specs(rows, count):
    return [
        pl.BlockSpec((rows, UNIT), lambda i, order, u=u: (0, order[4 * i + u])) for u in range(count)
    ]


def project(order, own, other, pieces, sums=None, tokens=()):
    rows = own.shape[0]
    count = len(pieces)
    last = sums is not None

    def kernel(order_ref, *refs):
        own_refs, other_refs, slabs = refs[:4], refs[4:8], refs[8 : 8 + count]
        rest = refs[8 + count :]
        step = pl.program_id(0)

        def part(columns, slab):
            total = jnp.dot(columns[0][...], slab[0], preferred_element_type=F32)
            for u in range(1, 4):
                total += jnp.dot(columns[u][...], slab[u], preferred_element_type=F32)
            return total

        if last:
            mine = rest[0][...] + part(own_refs, slabs[0])
            theirs = rest[1][...] + part(other_refs, slabs[0])
            rest[4][...] = mine
            rest[5][...] = mine.astype(BF)
            rest[6][...] = theirs.astype(BF)
            squares = jnp.sum(mine * mine + theirs * theirs, axis=0, keepdims=True)
            low, high = (jnp.concatenate([squares[:, at : at + 128]] * 4, 1) for at in (0, 128))
            line = lax.broadcasted_iota(jnp.int32, (16, UNIT), 0)
            squares = jnp.where(line == 0, low, jnp.where(line == 1, high, 0.0)).astype(BF)
            product = jnp.dot(rest[2][...], rest[5][...], preferred_element_type=F32)
            product += jnp.dot(rest[3][...], rest[6][...], preferred_element_type=F32)
            for u in range(16):
                eight = [product[at : at + 8] for at in range(32 * u, 32 * u + 32, 8)]
                eight = [jnp.concatenate([e[:, :128], e[:, 128:]], 0) for e in eight]
                rest[7][u, :16] = squares
                rest[7][u, 16:] = jnp.concatenate(eight, 1).astype(BF)
            return
        for k, slab in enumerate(slabs):

            @pl.when(step == k)
            def _(slab=slab, k=k):
                mine, theirs = part(own_refs, slab), part(other_refs, slab)
                rest[0][...] = mine if k == 0 else rest[0][...] + mine
                rest[1][...] = theirs if k == 0 else rest[1][...] + theirs

    whole = pl.BlockSpec((rows, HALF), lambda i, order: (0, 0))
    slab_spec = pl.BlockSpec((4, UNIT, HALF), lambda i, order: (0, 0, 0))
    shape = lambda dtype: jax.ShapeDtypeStruct((rows, HALF), dtype)
    in_specs = column_specs(rows, 4) * 2 + [slab_spec] * count
    out_specs, out_shape = [whole, whole], [shape(F32), shape(F32)]
    if last:
        in_specs += [whole, whole] + [pl.BlockSpec(t.shape, lambda i, order: (0, 0)) for t in tokens]
        out_specs = [whole, whole, whole, pl.BlockSpec((16, 32, UNIT), lambda i, order: (0, 0, 0))]
        out_shape = [shape(F32), shape(BF), shape(BF), jax.ShapeDtypeStruct((16, 32, UNIT), BF)]
    return pl.pallas_call(
        kernel,
        grid_spec=pltpu.PrefetchScalarGridSpec(
            num_scalar_prefetch=1, grid=(count,), in_specs=in_specs, out_specs=out_specs
        ),
        out_shape=out_shape,
        compiler_params=params(),
    )(order, *([own] * 4), *([other] * 4), *pieces, *(sums or ()), *tokens)


def project_back(order, own, other, p_own, p_other, below):
    rows = own.shape[0]
    count = order.shape[0] // 4

    def kernel(order_ref, *refs):
        own_refs, other_refs, below_refs, outs = refs[:4], refs[4:8], refs[10:14], refs[14:]
        p_own_ref, p_other_ref = refs[8:10]
        step = pl.program_id(0)
        for k, out in enumerate(outs):

            @pl.when(step == k)
            def _(out=out):
                left_own, left_other = jnp.transpose(p_own_ref[...]), jnp.transpose(p_other_ref[...])
                for u in range(4):
                    value = jnp.dot(left_own, own_refs[u][...], preferred_element_type=F32)
                    value += jnp.dot(left_other, other_refs[u][...], preferred_element_type=F32)
                    out[u, :HALF] = value.astype(BF)
                    out[u, HALF:] = below_refs[u][0]

    whole = pl.BlockSpec((rows, HALF), lambda i, order: (0, 0))
    return pl.pallas_call(
        kernel,
        grid_spec=pltpu.PrefetchScalarGridSpec(
            num_scalar_prefetch=1,
            grid=(count,),
            in_specs=column_specs(rows, 4) * 2
            + [whole, whole]
            + [
                pl.BlockSpec((1, 32, UNIT), lambda i, order, u=u: (order[4 * i + u], 0, 0))
                for u in range(4)
            ],
            out_specs=[pl.BlockSpec((4, TALL, UNIT), lambda i, order: (0, 0, 0))] * count,
        ),
        out_shape=[jax.ShapeDtypeStruct((4, TALL, UNIT), BF)] * count,
        compiler_params=params(),
    )(order, *([own] * 4), *([other] * 4), p_own, p_other, *([below] * 4))


def update_momentum(order, units, momentum, gradient, left_own, left_other, q_own, q_other, tile=None):
    rows, width = momentum.shape
    count = len(units)
    chunks = 3
    parts_of = []
    for side, slabs in enumerate((q_own, q_other)):
        for k in sorted({unit[side] for unit in units}):
            at = 0
            for part in slabs[k]:
                parts_of.append((side, k, at, part))
                at += part.shape[0]

    def find(refs, side, k, j):
        for ref, (s, slab, at, part) in zip(refs, parts_of):
            if s == side and slab == k and at <= j < at + part.shape[0]:
                return ref.at[j - at, pl.ds(0, HALF)]

    def kernel(order_ref, lo_ref, lp_ref, m_ref, g_ref, *refs):
        *refs, left_all, left_sems = refs
        slab_refs, refs = refs[: len(parts_of)], refs[len(parts_of) :]
        if tile is not None:
            _, place_ref, f_ref, *small_refs, w_ref, po_ref, pp_ref = refs[:9]
            new_ref, logits_ref, basis_ref = refs[10:13]
            (early_ref, mine_ref, theirs_ref), refs_left = refs[-4:-1], refs[:-4]
            small_sems = refs[-1]
            w_all, p_all, w_out, unit, scaled, lines, w_sems, unit_sems, w_out_sems = refs_left[-9:]
            out_ref, refs = refs[9], refs_left[13:-9]
        else:
            out_ref, refs = refs[0], refs[1:]
        m_all, g_all, q_all, out_all, in_sems, out_sems = refs
        lefts = [
            pltpu.make_async_copy(a, left_all.at[:, pl.ds(n * HALF, HALF)], left_sems.at[n])
            for n, a in enumerate((lo_ref, lp_ref))
        ]
        for copy in lefts:
            copy.start()
        loads, stores = [], []
        for n, (k, j) in enumerate(units):
            columns = pl.ds(pl.multiple_of(order_ref[n] * UNIT, UNIT), UNIT)
            pairs = (
                (m_ref.at[:, columns], m_all.at[n]),
                (g_ref.at[:, columns], g_all.at[n]),
                (find(slab_refs, 0, k, j), q_all.at[n, pl.ds(0, HALF)]),
                (find(slab_refs, 1, j, k), q_all.at[n, pl.ds(HALF, HALF)]),
            )
            loads.append(
                [pltpu.make_async_copy(a, b, in_sems.at[n, i]) for i, (a, b) in enumerate(pairs)]
            )
            stores.append(pltpu.make_async_copy(out_all.at[n], out_ref.at[:, columns], out_sems.at[n]))
        for copies in loads:
            for copy in copies:
                copy.start()
        if tile is not None:
            small = [
                pltpu.make_async_copy(a, b, small_sems.at[n])
                for n, (a, b) in enumerate(zip(small_refs, (early_ref, mine_ref, theirs_ref)))
            ]
            for copy in small:
                copy.start()
            wanted = [
                [
                    (0, pl.ds(0, HALF), unit.at[side]),
                    (2, pl.ds(HALF + 16, 16), lines.at[side, 0]),
                    (4, pl.ds(HALF + 16, 16), lines.at[side, 1]),
                ]
                for side in range(2)
            ]
            for ref, (side, k, start, values) in zip(slab_refs, parts_of):
                for n, (at, part, target) in enumerate(wanted[side]):
                    near = place_ref[at + 1 - side]
                    here = (place_ref[at + side] == k) & (near >= start)

                    @pl.when(here & (near < start + values.shape[0]))
                    def _(ref=ref, side=side, start=start, n=n, part=part, target=target, near=near):
                        source = ref.at[near - start, part]
                        pltpu.make_async_copy(source, target, unit_sems.at[side, n]).start()

            chunk = w_ref.shape[0] // chunks
            parts = [pl.ds(i * chunk, chunk) for i in range(chunks)]
            targets = (
                (w_ref, w_all),
                (po_ref, p_all.at[:, pl.ds(0, HALF)]),
                (pp_ref, p_all.at[:, pl.ds(HALF, HALF)]),
            )
            w_loads = [
                [
                    pltpu.make_async_copy(a.at[part], b.at[part], w_sems.at[i, n])
                    for n, (a, b) in enumerate(targets)
                ]
                for i, part in enumerate(parts)
            ]
            w_stores = [
                pltpu.make_async_copy(w_out.at[part], new_ref.at[part], w_out_sems.at[i])
                for i, part in enumerate(parts)
            ]
            for copies in w_loads:
                for copy in copies:
                    copy.start()
        for copy in lefts:
            copy.wait()
        left = left_all[...]
        for n in range(count):
            for copy in loads[n]:
                copy.wait()
            change = jnp.dot(left, q_all[n], preferred_element_type=F32)
            out_all[n] = (m_all[n] + g_all[n].astype(F32)) - (1.0 - MOMENTUM_DECAY) * change
            stores[n].start()
        if tile is not None:
            for copy in small:
                copy.wait()
            core = pl.multiple_of(place_ref[6] * HALF, HALF)
            basis_ref[:, pl.ds(core, HALF)] = (mine_ref[...].astype(F32) * f_ref[2:3]).astype(BF)
            basis_ref[:, pl.ds(HALF - core, HALF)] = (
                theirs_ref[...].astype(F32) * f_ref[3:4]
            ).astype(BF)
            late = 0.0
            for side in range(2):
                for n, (_, part, target) in enumerate(wanted[side]):
                    pltpu.make_async_copy(slab_refs[0].at[0, part], target, unit_sems.at[side, n]).wait()
                factor = jnp.transpose(jnp.broadcast_to(f_ref[side : side + 1], (128, HALF)))
                for at in range(0, UNIT, 128):
                    columns = slice(at, at + 128)
                    scaled[side * HALF : side * HALF + HALF, columns] = (
                        unit[side, :, columns].astype(F32) * factor
                    ).astype(BF)
                product = []
                for half in range(2):
                    block = lines[side, half].astype(F32)
                    for at in range(0, UNIT, 128):
                        eight = block[:, at : at + 128]
                        product.append(jnp.concatenate([eight[:8], eight[8:]], 1))
                product = jnp.concatenate(product, 0).astype(BF)
                late += jnp.dot(product, scaled[side * HALF : side * HALF + HALF], preferred_element_type=F32)
            logits_ref[...] = ((early_ref[...].astype(F32) - late) * tile[-1]).astype(BF)
            for i, part in enumerate(parts):
                for copy in w_loads[i]:
                    copy.wait()
                change = jnp.dot(p_all[part, :], scaled[...], preferred_element_type=F32)
                w_out[part, :] = (w_all[part, :].astype(F32) - change).astype(BF)
                w_stores[i].start()
            for copy in w_stores:
                copy.wait()
        for copy in stores:
            copy.wait()

    anywhere = pl.BlockSpec(memory_space=pl.ANY)
    vmem = pl.BlockSpec(memory_space=pltpu.VMEM)
    smem = pl.BlockSpec(memory_space=pltpu.SMEM)
    operands = [order, *map(in_hbm, (left_own, left_other, momentum, gradient))]
    in_specs = [smem, anywhere, anywhere, anywhere, anywhere]
    operands += [part for *_, part in parts_of]
    in_specs += [anywhere] * len(parts_of)
    out_specs, out_shape = [anywhere], [jax.ShapeDtypeStruct((rows, width), F32)]
    scratch_shapes = [
        pltpu.VMEM((count, rows, UNIT), F32),
        pltpu.VMEM((count, rows, UNIT), BF),
        pltpu.VMEM((count, 2 * HALF, UNIT), BF),
        pltpu.VMEM((count, rows, UNIT), F32),
        pltpu.SemaphoreType.DMA((count, 4)),
        pltpu.SemaphoreType.DMA((count,)),
    ]
    aliases = {}
    if tile is not None:
        aliases = {len(operands): 0}
        operands += [in_hbm(tile[0]), *tile[1:3], *map(in_hbm, tile[3:7]), *tile[7:-1]]
        in_specs += [anywhere, smem, vmem] + [anywhere] * 6
        tall, tokens = tile[6].shape[0], tile[3].shape[0]
        out_specs += [anywhere, vmem, vmem]
        out_shape += [
            jax.ShapeDtypeStruct((tall, UNIT), BF),
            jax.ShapeDtypeStruct((tokens, UNIT), BF),
            jax.ShapeDtypeStruct((tokens, UNIT), BF),
        ]
        scratch_shapes += [
            pltpu.VMEM((tall, UNIT), BF),
            pltpu.VMEM((tall, 2 * HALF), BF),
            pltpu.VMEM((tall, UNIT), BF),
            pltpu.VMEM((2, HALF, UNIT), BF),
            pltpu.VMEM((2 * HALF, UNIT), BF),
            pltpu.VMEM((2, 2, 16, UNIT), BF),
            pltpu.SemaphoreType.DMA((chunks, 3)),
            pltpu.SemaphoreType.DMA((2, 3)),
            pltpu.SemaphoreType.DMA((chunks,)),
            pltpu.VMEM((tokens, UNIT), BF),
            pltpu.VMEM((tokens, HALF), BF),
            pltpu.VMEM((tokens, HALF), BF),
            pltpu.SemaphoreType.DMA((3,)),
        ]
    scratch_shapes += [pltpu.VMEM((rows, 2 * HALF), BF), pltpu.SemaphoreType.DMA((2,))]
    return pl.pallas_call(
        kernel,
        in_specs=in_specs,
        out_specs=out_specs,
        out_shape=out_shape,
        scratch_shapes=scratch_shapes,
        input_output_aliases=aliases,
        compiler_params=params(),
    )(*operands)


def sum_squares(parts):
    def kernel(*refs):
        total = sum(ref[u].astype(F32) for ref in refs[:-1] for u in range(ref.shape[0]))
        total = sum(total[:, at : at + 128] for at in range(0, UNIT, 128))
        refs[-1][...] = total[0:2] + total[2:4] + total[4:6]

    return pl.pallas_call(
        kernel,
        grid=(1,),
        in_specs=[pl.BlockSpec((p.shape[0], 16, UNIT), lambda i: (0, HALF // 16, 0)) for p in parts],
        out_specs=pl.BlockSpec((2, 128), lambda i: (0, 0)),
        out_shape=jax.ShapeDtypeStruct((2, 128), F32),
        compiler_params=params(),
    )(*parts)


def three_terms(value):
    high = value.astype(BF)
    rest = value - high.astype(F32)
    middle = rest.astype(BF)
    return jnp.stack([high, middle, (rest - middle.astype(F32)).astype(BF)])


def shards(momentum, gradient, right_basis, weight, tokens):
    row, col = lax.axis_index("row"), lax.axis_index("col")
    x, y, z, core = row // 2, (col // 8) * 2 + row % 2, (col // 2) % 4, col % 2
    first = core == 0
    total_rows = momentum.shape[0] * 128
    rank = right_basis.shape[1]
    width = momentum.shape[1]
    rows = momentum.shape[0]
    big, middle = ("x", "y"), ("y", "x")
    deep = ("z", "z")

    def unit_at(k, j):
        ux = jnp.where(first, x + k, x + j) % 4
        uy = jnp.where(first, y + j, y + k) % 4
        return ux * 4 + (uy % 2) * 2 + uy // 2

    def orders(units):
        return jnp.stack([unit_at(k, j) for k, j in units]).astype(jnp.int32)

    def slab_orders(*slabs):
        return orders([(k, j) for k in slabs for j in range(4)])

    def halves(a):
        low, high = a[:, :HALF], a[:, HALF:]
        return jnp.where(first, low, high), jnp.where(first, high, low)

    def by_core(mine, theirs):
        return jnp.where(first, mine, theirs), jnp.where(first, theirs, mine)

    def by_half(mine, theirs):
        low = y < 2
        return jnp.stack([jnp.where(low, mine, theirs), jnp.where(low, theirs, mine)])

    def swap_y_hi(value):
        return shift_by(value, ("y", "y"), 2)

    def pick(bit, values):
        return jnp.where(bit == 0, values[0], values[1]), jnp.where(bit == 0, values[1], values[0])

    basis_own, basis_sent = halves(right_basis)
    basis_other = swap_cores(basis_sent)
    basis_chip = jnp.concatenate(by_core(basis_own, basis_other), 0)
    stack = jnp.stack(gather_ring(basis_chip, deep))
    unit = rotate(stack, (4 - z) % 4).reshape(UNIT, HALF)
    tokens_near = swap_y_hi(tokens)
    unit, tokens_near = lax.optimization_barrier((unit, tokens_near))

    momentum_in, gradient_in, _ = lax.optimization_barrier((momentum, gradient, unit))
    buffer_low = (momentum_in + gradient_in.astype(F32)).astype(BF)
    slab = jnp.stack(gather_ring(unit, middle))
    slab, buffer_sent = lax.optimization_barrier((slab, buffer_low))
    pieces = gather_ring(slab, big)
    buffer_other = swap_cores(buffer_sent)

    tokens_all = lax.all_gather(
        by_half(tokens, tokens_near).reshape(64, -1), "col", axis=0,
        axis_index_groups=[[8 * k + i for i in range(8)] for k in range(2)], tiled=True,
    )
    token_parts = [
        lax.dynamic_slice_in_dim(tokens_all, rows * c, rows, 1) for c in (col, col ^ 1)
    ]

    early = jnp.dot(tokens_all, weight, preferred_element_type=F32).astype(BF)
    early = early.reshape(2, 2, 2, 2, 32, -1)
    pieces[3], early, *token_parts = lax.optimization_barrier((pieces[3], early, *token_parts))

    def halve(value, bit, send):
        kept, sent = pick(bit, value)
        return (kept.astype(F32) + send(sent).astype(F32)).astype(BF)

    sums = project(slab_orders(0, 1, 3), buffer_low, buffer_other, [pieces[0], pieces[1], pieces[3]])
    p_own, p_own_low, p_other, below = project(
        slab_orders(2), buffer_low, buffer_other, [pieces[2]], sums, token_parts
    )

    p_chip = jnp.stack(by_core(p_own_low, p_other))
    p_far = swap_y_hi(p_chip)
    p_pair = by_half(p_chip, p_far)

    slabs = [None] * 4
    (slabs[2],) = project_back(slab_orders(2), buffer_low, buffer_other, p_own_low, p_other, below)
    slabs[1], slabs[3] = project_back(
        after(slab_orders(1, 3), slabs[2]), buffer_low, buffer_other, p_own_low, p_other, below
    )
    (slabs[0],) = project_back(after(slab_orders(0), slabs[1]), buffer_low, buffer_other, p_own_low, p_other, below)
    summed = scatter_ring(slabs, big, (p_pair,)).astype(BF)
    p_tile = gather_z(p_pair[None])
    early = halve((early[:, 0], early[:, 1]), row % 2, lambda v: swap_y_lo(after(v, summed)))
    summed = scatter_ring([summed[k] for k in range(4)], middle, (early,)).astype(BF)
    early = halve((early[0], early[1]), x % 2, lambda v: exchange(after(v, summed), "x", 1))
    summed = summed.reshape(TALL, 4, 128).transpose(1, 0, 2)
    summed = rotate(summed, z)
    summed = scatter_ring([summed[k] for k in range(4)], deep, (early,))
    early = halve((early[:, 0], early[:, 1]), x // 2, lambda v: exchange(after(v, summed), "x", 2))
    early = early.reshape(64, -1)
    q_block = summed[:HALF].astype(BF)
    scale = lax.rsqrt(summed[HALF : HALF + 2].reshape(HALF) + EPSILON)

    p_tile = after(p_tile, q_block).transpose(1, 0, 2, 3, 4).reshape(16 * rows, HALF)

    left_part, right_part = q_block[:, :64].T, q_block[:, 64:].T
    mine = jnp.where(first, left_part, right_part)
    theirs = swap_cores(jnp.where(first, right_part, left_part))
    squared = scale * scale
    left_own = (p_own * squared).astype(BF)
    left_other = swap_cores((p_other.astype(F32) * squared).astype(BF))

    q_wide = q_block.astype(F32)
    terms = three_terms(jnp.sum(q_wide * q_wide, axis=1)).reshape(6, 128)
    block = jnp.concatenate([q_block, jnp.pad(terms, ((0, 10), (0, 0))), summed[HALF + 16 :].astype(BF)], 0)
    stack = rotate(jnp.stack(gather_ring(block, deep)), (4 - z) % 4)
    unit = stack.transpose(1, 0, 2).reshape(TALL, UNIT)
    unit, mine, theirs, left_own, left_other, early = lax.optimization_barrier(
        (unit, mine, theirs, left_own, left_other, early)
    )
    slab = jnp.stack(gather_ring(unit, middle))
    q_ahead, q_before = shift_by(slab, big, -1), shift_by(slab, big, 1)
    q_ahead, p_tile = lax.optimization_barrier((q_ahead, p_tile))
    q_across = [shift_by(q_ahead[:2], big, -1), shift_by(q_before[2:], big, 1)]
    p_tile_other = swap_cores(p_tile)
    q_own = [[slab], [q_ahead], q_across, [q_before]]
    q_other = [[swap_cores(part) for part in q_own[k]] if k != 2 else None for k in range(4)]

    near = [(k, j) for k in (0, 1, 3) for j in (0, 1, 3)]
    across = [(2, 0), (2, 1), (2, 3), (0, 2), (1, 2), (3, 2), (2, 2)]
    (new_momentum,) = update_momentum(
        orders(near), near, momentum, gradient, left_own, left_other, q_own, q_other
    )
    *q_own[2], _ = lax.optimization_barrier((*q_own[2], new_momentum))
    q_other[2] = [swap_cores(part) for part in q_own[2]]
    squares = sum_squares([part for parts in q_own for part in parts]).reshape(HALF)
    basis_scale = lax.rsqrt(squared * squares + EPSILON)
    factors = jnp.stack([squared * basis_scale, scale * basis_scale])
    factors_other = swap_cores(factors)

    def place_of(unit):
        dx, dy = (unit // 4 - x) % 4, ((unit % 2) * 2 + (unit // 2) % 2 - y) % 4
        return [jnp.where(first, dx, dy), jnp.where(first, dy, dx)]

    block = (row % 4) * 4 + row // 4
    place = place_of(col) + place_of(block) + place_of(block + 2) + [core]
    step_scale = STEP_SIZE * math.sqrt(total_rows * width / rank)
    factors, factors_other = factors * jnp.array([[step_scale], [1.0]], F32), factors_other * jnp.array(
        [[step_scale], [1.0]], F32
    )
    tile = [
        new_momentum,
        jnp.stack(place).astype(jnp.int32),
        jnp.stack([factors[0], factors_other[0], factors[1], factors_other[1]]),
        early,
        mine,
        theirs,
        weight,
        p_tile,
        p_tile_other,
        total_rows ** (-0.5),
    ]
    new_momentum, new_weight, logits, new_basis = update_momentum(
        orders(across), across, momentum, gradient, left_own, left_other, q_own, q_other, tile
    )
    return (new_momentum, new_basis, new_weight, logits)


def solution(mesh):
    in_specs = (
        P(("row", "col"), None),
        P(("row", "col"), None),
        P(("row", "col"), None),
        P("row", "col"),
        P("col", "row"),
    )
    out_specs = (P(("row", "col"), None), P(("row", "col"), None), P("row", "col"), P("row", "col"))
    return jax.shard_map(shards, mesh=mesh, in_specs=in_specs, out_specs=out_specs, check_vma=False)
```

```python
import math

import jax
import jax.numpy as jnp
from jax import lax
from jax.experimental import pallas as pl
from jax.experimental.pallas import tpu as pltpu
from jax.sharding import PartitionSpec as P

EPSILON = 1e-06
MOMENTUM_DECAY = 0.95
STEP_SIZE = 0.3
BF = jnp.bfloat16
F32 = jnp.float32
ALL = ("row", "col")
VMEM_LIMIT = 28 * 1024 * 1024
HALF = 256
TALL = HALF + 32
UNIT = 512


def device_id(x, y, z, core):
    x, y, z = x % 4, y % 4, z % 4
    return (x * 2 + y % 2) * 16 + (y // 2) * 8 + z * 2 + core


def places():
    return [(x, y, z, c) for x in range(4) for y in range(4) for z in range(4) for c in range(2)]


def moved(place, axis, shift):
    place = list(place)
    place["xyz".index(axis)] += shift
    return device_id(*place)


def shift_by(value, axes, shift):
    pairs = [(device_id(*p), moved(p, axes[p[3]], shift)) for p in places()]
    return lax.ppermute(value, ALL, pairs)


def gather_z(value):
    groups = [[y * 8 + z * 2 + c for z in range(4)] for y in range(2) for c in range(2)]
    return lax.all_gather(value, "col", axis=0, axis_index_groups=groups, tiled=True)


def exchange(value, axis, distance):
    pairs = []
    for p in places():
        other = list(p)
        other["xyz".index(axis)] ^= distance
        pairs.append((device_id(*p), device_id(*other)))
    return lax.ppermute(value, ALL, pairs)


def swap_y_lo(value):
    return exchange(value, "y", 1)


def swap_cores(value):
    return lax.ppermute(value, ALL, [(i, i ^ 1) for i in range(128)])


def gather_ring(block, axes, far_block=None):
    ahead = shift_by(block, axes, -1)
    before = shift_by(block, axes, 1)
    across = shift_by(block if far_block is None else far_block, axes, 2)
    return [block, ahead, across, before]


def scatter_ring(blocks, axes, done=None):
    from_before = shift_by(blocks[1], axes, 1)
    from_after = shift_by(blocks[3], axes, -1)
    from_across = shift_by(blocks[2], axes, 2)
    if done is not None:
        from_across = after(from_across, *done)
    return (
        (blocks[0].astype(F32) + from_across.astype(F32))
        + (from_before.astype(F32) + from_after.astype(F32))
    )


def rotate(stack, start):
    return lax.dynamic_slice_in_dim(jnp.concatenate([stack, stack], 0), start, 4, 0)


def in_hbm(value):
    return pltpu.with_memory_space_constraint(value, pltpu.HBM)


def after(value, *done):
    return lax.optimization_barrier((value, *done))[0]


def params():
    return pltpu.CompilerParams(vmem_limit_bytes=VMEM_LIMIT)


def column_specs(rows, count):
    return [
        pl.BlockSpec((rows, UNIT), lambda i, order, u=u: (0, order[4 * i + u])) for u in range(count)
    ]


def project(order, own, other, pieces, sums=None, tokens=()):
    rows = own.shape[0]
    count = len(pieces)
    last = sums is not None

    def kernel(order_ref, *refs):
        own_refs, other_refs, slabs = refs[:4], refs[4:8], refs[8 : 8 + count]
        rest = refs[8 + count :]
        step = pl.program_id(0)

        def part(columns, slab):
            total = jnp.dot(columns[0][...], slab[0], preferred_element_type=F32)
            for u in range(1, 4):
                total += jnp.dot(columns[u][...], slab[u], preferred_element_type=F32)
            return total

        if last:
            mine = rest[0][...] + part(own_refs, slabs[0])
            theirs = rest[1][...] + part(other_refs, slabs[0])
            rest[4][...] = mine
            rest[5][...] = mine.astype(BF)
            rest[6][...] = theirs.astype(BF)
            squares = jnp.sum(mine * mine + theirs * theirs, axis=0, keepdims=True)
            low, high = (jnp.concatenate([squares[:, at : at + 128]] * 4, 1) for at in (0, 128))
            line = lax.broadcasted_iota(jnp.int32, (16, UNIT), 0)
            squares = jnp.where(line == 0, low, jnp.where(line == 1, high, 0.0)).astype(BF)
            product = jnp.dot(rest[2][...], rest[5][...], preferred_element_type=F32)
            product += jnp.dot(rest[3][...], rest[6][...], preferred_element_type=F32)
            for u in range(16):
                eight = [product[at : at + 8] for at in range(32 * u, 32 * u + 32, 8)]
                eight = [jnp.concatenate([e[:, :128], e[:, 128:]], 0) for e in eight]
                rest[7][u, :16] = squares
                rest[7][u, 16:] = jnp.concatenate(eight, 1).astype(BF)
            return
        for k, slab in enumerate(slabs):

            @pl.when(step == k)
            def _(slab=slab, k=k):
                mine, theirs = part(own_refs, slab), part(other_refs, slab)
                rest[0][...] = mine if k == 0 else rest[0][...] + mine
                rest[1][...] = theirs if k == 0 else rest[1][...] + theirs

    whole = pl.BlockSpec((rows, HALF), lambda i, order: (0, 0))
    slab_spec = pl.BlockSpec((4, UNIT, HALF), lambda i, order: (0, 0, 0))
    shape = lambda dtype: jax.ShapeDtypeStruct((rows, HALF), dtype)
    in_specs = column_specs(rows, 4) * 2 + [slab_spec] * count
    out_specs, out_shape = [whole, whole], [shape(F32), shape(F32)]
    if last:
        in_specs += [whole, whole] + [pl.BlockSpec(t.shape, lambda i, order: (0, 0)) for t in tokens]
        out_specs = [whole, whole, whole, pl.BlockSpec((16, 32, UNIT), lambda i, order: (0, 0, 0))]
        out_shape = [shape(F32), shape(BF), shape(BF), jax.ShapeDtypeStruct((16, 32, UNIT), BF)]
    return pl.pallas_call(
        kernel,
        grid_spec=pltpu.PrefetchScalarGridSpec(
            num_scalar_prefetch=1, grid=(count,), in_specs=in_specs, out_specs=out_specs
        ),
        out_shape=out_shape,
        compiler_params=params(),
    )(order, *([own] * 4), *([other] * 4), *pieces, *(sums or ()), *tokens)


def project_back(order, own, other, p_own, p_other, below):
    rows = own.shape[0]
    count = order.shape[0] // 4

    def kernel(order_ref, *refs):
        own_refs, other_refs, below_refs, outs = refs[:4], refs[4:8], refs[10:14], refs[14:]
        p_own_ref, p_other_ref = refs[8:10]
        step = pl.program_id(0)
        for k, out in enumerate(outs):

            @pl.when(step == k)
            def _(out=out):
                left_own, left_other = jnp.transpose(p_own_ref[...]), jnp.transpose(p_other_ref[...])
                for u in range(4):
                    value = jnp.dot(left_own, own_refs[u][...], preferred_element_type=F32)
                    value += jnp.dot(left_other, other_refs[u][...], preferred_element_type=F32)
                    out[u, :HALF] = value.astype(BF)
                    out[u, HALF:] = below_refs[u][0]

    whole = pl.BlockSpec((rows, HALF), lambda i, order: (0, 0))
    return pl.pallas_call(
        kernel,
        grid_spec=pltpu.PrefetchScalarGridSpec(
            num_scalar_prefetch=1,
            grid=(count,),
            in_specs=column_specs(rows, 4) * 2
            + [whole, whole]
            + [
                pl.BlockSpec((1, 32, UNIT), lambda i, order, u=u: (order[4 * i + u], 0, 0))
                for u in range(4)
            ],
            out_specs=[pl.BlockSpec((4, TALL, UNIT), lambda i, order: (0, 0, 0))] * count,
        ),
        out_shape=[jax.ShapeDtypeStruct((4, TALL, UNIT), BF)] * count,
        compiler_params=params(),
    )(order, *([own] * 4), *([other] * 4), p_own, p_other, *([below] * 4))


def update_momentum(order, units, momentum, gradient, left_own, left_other, q_own, q_other, tile=None):
    rows, width = momentum.shape
    count = len(units)
    chunks = 3
    parts_of = []
    for side, slabs in enumerate((q_own, q_other)):
        for k in sorted({unit[side] for unit in units}):
            at = 0
            for part in slabs[k]:
                parts_of.append((side, k, at, part))
                at += part.shape[0]

    def find(refs, side, k, j):
        for ref, (s, slab, at, part) in zip(refs, parts_of):
            if s == side and slab == k and at <= j < at + part.shape[0]:
                return ref.at[j - at, pl.ds(0, HALF)]

    def kernel(order_ref, lo_ref, lp_ref, m_ref, g_ref, *refs):
        *refs, left_all, left_sems = refs
        slab_refs, refs = refs[: len(parts_of)], refs[len(parts_of) :]
        if tile is not None:
            _, place_ref, f_ref, *small_refs, w_ref, po_ref, pp_ref = refs[:9]
            new_ref, logits_ref, basis_ref = refs[10:13]
            (early_ref, mine_ref, theirs_ref), refs_left = refs[-4:-1], refs[:-4]
            small_sems = refs[-1]
            w_all, p_all, w_out, unit, scaled, lines, w_sems, unit_sems, w_out_sems = refs_left[-9:]
            out_ref, refs = refs[9], refs_left[13:-9]
        else:
            out_ref, refs = refs[0], refs[1:]
        m_all, g_all, q_all, out_all, in_sems, out_sems = refs
        lefts = [
            pltpu.make_async_copy(a, left_all.at[:, pl.ds(n * HALF, HALF)], left_sems.at[n])
            for n, a in enumerate((lo_ref, lp_ref))
        ]
        for copy in lefts:
            copy.start()
        loads, stores = [], []
        for n, (k, j) in enumerate(units):
            columns = pl.ds(pl.multiple_of(order_ref[n] * UNIT, UNIT), UNIT)
            pairs = (
                (m_ref.at[:, columns], m_all.at[n]),
                (g_ref.at[:, columns], g_all.at[n]),
                (find(slab_refs, 0, k, j), q_all.at[n, pl.ds(0, HALF)]),
                (find(slab_refs, 1, j, k), q_all.at[n, pl.ds(HALF, HALF)]),
            )
            loads.append(
                [pltpu.make_async_copy(a, b, in_sems.at[n, i]) for i, (a, b) in enumerate(pairs)]
            )
            stores.append(pltpu.make_async_copy(out_all.at[n], out_ref.at[:, columns], out_sems.at[n]))
        for copies in loads:
            for copy in copies:
                copy.start()
        if tile is not None:
            small = [
                pltpu.make_async_copy(a, b, small_sems.at[n])
                for n, (a, b) in enumerate(zip(small_refs, (early_ref, mine_ref, theirs_ref)))
            ]
            for copy in small:
                copy.start()
            wanted = [
                [
                    (0, pl.ds(0, HALF), unit.at[side]),
                    (2, pl.ds(HALF + 16, 16), lines.at[side, 0]),
                    (4, pl.ds(HALF + 16, 16), lines.at[side, 1]),
                ]
                for side in range(2)
            ]
            for ref, (side, k, start, values) in zip(slab_refs, parts_of):
                for n, (at, part, target) in enumerate(wanted[side]):
                    near = place_ref[at + 1 - side]
                    here = (place_ref[at + side] == k) & (near >= start)

                    @pl.when(here & (near < start + values.shape[0]))
                    def _(ref=ref, side=side, start=start, n=n, part=part, target=target, near=near):
                        source = ref.at[near - start, part]
                        pltpu.make_async_copy(source, target, unit_sems.at[side, n]).start()

            chunk = w_ref.shape[0] // chunks
            parts = [pl.ds(i * chunk, chunk) for i in range(chunks)]
            targets = (
                (w_ref, w_all),
                (po_ref, p_all.at[:, pl.ds(0, HALF)]),
                (pp_ref, p_all.at[:, pl.ds(HALF, HALF)]),
            )
            w_loads = [
                [
                    pltpu.make_async_copy(a.at[part], b.at[part], w_sems.at[i, n])
                    for n, (a, b) in enumerate(targets)
                ]
                for i, part in enumerate(parts)
            ]
            w_stores = [
                pltpu.make_async_copy(w_out.at[part], new_ref.at[part], w_out_sems.at[i])
                for i, part in enumerate(parts)
            ]
            for copies in w_loads:
                for copy in copies:
                    copy.start()
        for copy in lefts:
            copy.wait()
        left = left_all[...]
        for n in range(count):
            for copy in loads[n]:
                copy.wait()
            change = jnp.dot(left, q_all[n], preferred_element_type=F32)
            out_all[n] = (m_all[n] + g_all[n].astype(F32)) - (1.0 - MOMENTUM_DECAY) * change
            stores[n].start()
        if tile is not None:
            for copy in small:
                copy.wait()
            core = pl.multiple_of(place_ref[6] * HALF, HALF)
            basis_ref[:, pl.ds(core, HALF)] = (mine_ref[...].astype(F32) * f_ref[2:3]).astype(BF)
            basis_ref[:, pl.ds(HALF - core, HALF)] = (
                theirs_ref[...].astype(F32) * f_ref[3:4]
            ).astype(BF)
            late = 0.0
            for side in range(2):
                for n, (_, part, target) in enumerate(wanted[side]):
                    pltpu.make_async_copy(slab_refs[0].at[0, part], target, unit_sems.at[side, n]).wait()
                factor = jnp.transpose(jnp.broadcast_to(f_ref[side : side + 1], (128, HALF)))
                for at in range(0, UNIT, 128):
                    columns = slice(at, at + 128)
                    scaled[side * HALF : side * HALF + HALF, columns] = (
                        unit[side, :, columns].astype(F32) * factor
                    ).astype(BF)
                product = []
                for half in range(2):
                    block = lines[side, half].astype(F32)
                    for at in range(0, UNIT, 128):
                        eight = block[:, at : at + 128]
                        product.append(jnp.concatenate([eight[:8], eight[8:]], 1))
                product = jnp.concatenate(product, 0).astype(BF)
                late += jnp.dot(product, scaled[side * HALF : side * HALF + HALF], preferred_element_type=F32)
            logits_ref[...] = ((early_ref[...].astype(F32) - late) * tile[-1]).astype(BF)
            for i, part in enumerate(parts):
                for copy in w_loads[i]:
                    copy.wait()
                change = jnp.dot(p_all[part, :], scaled[...], preferred_element_type=F32)
                w_out[part, :] = (w_all[part, :].astype(F32) - change).astype(BF)
                w_stores[i].start()
            for copy in w_stores:
                copy.wait()
        for copy in stores:
            copy.wait()

    anywhere = pl.BlockSpec(memory_space=pl.ANY)
    vmem = pl.BlockSpec(memory_space=pltpu.VMEM)
    smem = pl.BlockSpec(memory_space=pltpu.SMEM)
    operands = [order, *map(in_hbm, (left_own, left_other, momentum, gradient))]
    in_specs = [smem, anywhere, anywhere, anywhere, anywhere]
    operands += [part for *_, part in parts_of]
    in_specs += [anywhere] * len(parts_of)
    out_specs, out_shape = [anywhere], [jax.ShapeDtypeStruct((rows, width), F32)]
    scratch_shapes = [
        pltpu.VMEM((count, rows, UNIT), F32),
        pltpu.VMEM((count, rows, UNIT), BF),
        pltpu.VMEM((count, 2 * HALF, UNIT), BF),
        pltpu.VMEM((count, rows, UNIT), F32),
        pltpu.SemaphoreType.DMA((count, 4)),
        pltpu.SemaphoreType.DMA((count,)),
    ]
    aliases = {}
    if tile is not None:
        aliases = {len(operands): 0}
        operands += [in_hbm(tile[0]), *tile[1:3], *map(in_hbm, tile[3:7]), *tile[7:-1]]
        in_specs += [anywhere, smem, vmem] + [anywhere] * 6
        tall, tokens = tile[6].shape[0], tile[3].shape[0]
        out_specs += [anywhere, vmem, vmem]
        out_shape += [
            jax.ShapeDtypeStruct((tall, UNIT), BF),
            jax.ShapeDtypeStruct((tokens, UNIT), BF),
            jax.ShapeDtypeStruct((tokens, UNIT), BF),
        ]
        scratch_shapes += [
            pltpu.VMEM((tall, UNIT), BF),
            pltpu.VMEM((tall, 2 * HALF), BF),
            pltpu.VMEM((tall, UNIT), BF),
            pltpu.VMEM((2, HALF, UNIT), BF),
            pltpu.VMEM((2 * HALF, UNIT), BF),
            pltpu.VMEM((2, 2, 16, UNIT), BF),
            pltpu.SemaphoreType.DMA((chunks, 3)),
            pltpu.SemaphoreType.DMA((2, 3)),
            pltpu.SemaphoreType.DMA((chunks,)),
            pltpu.VMEM((tokens, UNIT), BF),
            pltpu.VMEM((tokens, HALF), BF),
            pltpu.VMEM((tokens, HALF), BF),
            pltpu.SemaphoreType.DMA((3,)),
        ]
    scratch_shapes += [pltpu.VMEM((rows, 2 * HALF), BF), pltpu.SemaphoreType.DMA((2,))]
    return pl.pallas_call(
        kernel,
        in_specs=in_specs,
        out_specs=out_specs,
        out_shape=out_shape,
        scratch_shapes=scratch_shapes,
        input_output_aliases=aliases,
        compiler_params=params(),
    )(*operands)


def sum_squares(parts):
    def kernel(*refs):
        total = sum(ref[u].astype(F32) for ref in refs[:-1] for u in range(ref.shape[0]))
        total = sum(total[:, at : at + 128] for at in range(0, UNIT, 128))
        refs[-1][...] = total[0:2] + total[2:4] + total[4:6]

    return pl.pallas_call(
        kernel,
        grid=(1,),
        in_specs=[pl.BlockSpec((p.shape[0], 16, UNIT), lambda i: (0, HALF // 16, 0)) for p in parts],
        out_specs=pl.BlockSpec((2, 128), lambda i: (0, 0)),
        out_shape=jax.ShapeDtypeStruct((2, 128), F32),
        compiler_params=params(),
    )(*parts)


def three_terms(value):
    high = value.astype(BF)
    rest = value - high.astype(F32)
    middle = rest.astype(BF)
    return jnp.stack([high, middle, (rest - middle.astype(F32)).astype(BF)])


def shards(momentum, gradient, right_basis, weight, tokens):
    row, col = lax.axis_index("row"), lax.axis_index("col")
    x, y, z, core = row // 2, (col // 8) * 2 + row % 2, (col // 2) % 4, col % 2
    first = core == 0
    total_rows = momentum.shape[0] * 128
    rank = right_basis.shape[1]
    width = momentum.shape[1]
    rows = momentum.shape[0]
    big, middle = ("x", "y"), ("y", "x")
    deep = ("z", "z")

    def unit_at(k, j):
        ux = jnp.where(first, x + k, x + j) % 4
        uy = jnp.where(first, y + j, y + k) % 4
        return ux * 4 + (uy % 2) * 2 + uy // 2

    def orders(units):
        return jnp.stack([unit_at(k, j) for k, j in units]).astype(jnp.int32)

    def slab_orders(*slabs):
        return orders([(k, j) for k in slabs for j in range(4)])

    def halves(a):
        low, high = a[:, :HALF], a[:, HALF:]
        return jnp.where(first, low, high), jnp.where(first, high, low)

    def by_core(mine, theirs):
        return jnp.where(first, mine, theirs), jnp.where(first, theirs, mine)

    def by_half(mine, theirs):
        low = y < 2
        return jnp.stack([jnp.where(low, mine, theirs), jnp.where(low, theirs, mine)])

    def swap_y_hi(value):
        return shift_by(value, ("y", "y"), 2)

    def pick(bit, values):
        return jnp.where(bit == 0, values[0], values[1]), jnp.where(bit == 0, values[1], values[0])

    basis_own, basis_sent = halves(right_basis)
    basis_other = swap_cores(basis_sent)
    basis_chip = jnp.concatenate(by_core(basis_own, basis_other), 0)
    stack = jnp.stack(gather_ring(basis_chip, deep))
    unit = rotate(stack, (4 - z) % 4).reshape(UNIT, HALF)
    tokens_near = swap_y_hi(tokens)
    unit, tokens_near = lax.optimization_barrier((unit, tokens_near))

    momentum_in, gradient_in, _ = lax.optimization_barrier((momentum, gradient, unit))
    buffer_low = (momentum_in + gradient_in.astype(F32)).astype(BF)
    slab = jnp.stack(gather_ring(unit, middle))
    slab, buffer_sent = lax.optimization_barrier((slab, buffer_low))
    pieces = gather_ring(slab, big)
    buffer_other = swap_cores(buffer_sent)

    tokens_all = lax.all_gather(
        by_half(tokens, tokens_near).reshape(64, -1), "col", axis=0,
        axis_index_groups=[[8 * k + i for i in range(8)] for k in range(2)], tiled=True,
    )
    token_parts = [
        lax.dynamic_slice_in_dim(tokens_all, rows * c, rows, 1) for c in (col, col ^ 1)
    ]

    early = jnp.dot(tokens_all, weight, preferred_element_type=F32).astype(BF)
    early = early.reshape(2, 2, 2, 2, 32, -1)
    pieces[3], early, *token_parts = lax.optimization_barrier((pieces[3], early, *token_parts))

    def halve(value, bit, send):
        kept, sent = pick(bit, value)
        return (kept.astype(F32) + send(sent).astype(F32)).astype(BF)

    sums = project(slab_orders(0, 1, 3), buffer_low, buffer_other, [pieces[0], pieces[1], pieces[3]])
    p_own, p_own_low, p_other, below = project(
        slab_orders(2), buffer_low, buffer_other, [pieces[2]], sums, token_parts
    )

    p_chip = jnp.stack(by_core(p_own_low, p_other))
    p_far = swap_y_hi(p_chip)
    p_pair = by_half(p_chip, p_far)

    slabs = [None] * 4
    (slabs[2],) = project_back(slab_orders(2), buffer_low, buffer_other, p_own_low, p_other, below)
    slabs[1], slabs[3] = project_back(
        after(slab_orders(1, 3), slabs[2]), buffer_low, buffer_other, p_own_low, p_other, below
    )
    (slabs[0],) = project_back(after(slab_orders(0), slabs[1]), buffer_low, buffer_other, p_own_low, p_other, below)
    summed = scatter_ring(slabs, big, (p_pair,)).astype(BF)
    p_tile = gather_z(p_pair[None])
    early = halve((early[:, 0], early[:, 1]), row % 2, lambda v: swap_y_lo(after(v, summed)))
    summed = scatter_ring([summed[k] for k in range(4)], middle, (early,)).astype(BF)
    early = halve((early[0], early[1]), x % 2, lambda v: exchange(after(v, summed), "x", 1))
    summed = summed.reshape(TALL, 4, 128).transpose(1, 0, 2)
    summed = rotate(summed, z)
    summed = scatter_ring([summed[k] for k in range(4)], deep, (early,))
    early = halve((early[:, 0], early[:, 1]), x // 2, lambda v: exchange(after(v, summed), "x", 2))
    early = early.reshape(64, -1)
    q_block = summed[:HALF].astype(BF)
    scale = lax.rsqrt(summed[HALF : HALF + 2].reshape(HALF) + EPSILON)

    p_tile = after(p_tile, q_block).transpose(1, 0, 2, 3, 4).reshape(16 * rows, HALF)

    left_part, right_part = q_block[:, :64].T, q_block[:, 64:].T
    mine = jnp.where(first, left_part, right_part)
    theirs = swap_cores(jnp.where(first, right_part, left_part))
    squared = scale * scale
    left_own = (p_own * squared).astype(BF)
    left_other = swap_cores((p_other.astype(F32) * squared).astype(BF))

    q_wide = q_block.astype(F32)
    terms = three_terms(jnp.sum(q_wide * q_wide, axis=1)).reshape(6, 128)
    block = jnp.concatenate([q_block, jnp.pad(terms, ((0, 10), (0, 0))), summed[HALF + 16 :].astype(BF)], 0)
    stack = rotate(jnp.stack(gather_ring(block, deep)), (4 - z) % 4)
    unit = stack.transpose(1, 0, 2).reshape(TALL, UNIT)
    unit, left_own, left_other, early = lax.optimization_barrier(
        (unit, left_own, left_other, early)
    )
    slab = jnp.stack(gather_ring(unit, middle))
    q_ahead, q_before = shift_by(slab, big, -1), shift_by(slab, big, 1)
    q_ahead, p_tile, mine, theirs = lax.optimization_barrier((q_ahead, p_tile, mine, theirs))
    q_across = [shift_by(q_ahead[:2], big, -1), shift_by(q_before[2:], big, 1)]
    p_tile_other = swap_cores(p_tile)
    q_own = [[slab], [q_ahead], q_across, [q_before]]
    q_other = [[swap_cores(part) for part in q_own[k]] if k != 2 else None for k in range(4)]

    near = [(k, j) for k in (0, 1, 3) for j in (0, 1, 3)]
    across = [(2, 0), (2, 1), (2, 3), (0, 2), (1, 2), (3, 2), (2, 2)]
    (new_momentum,) = update_momentum(
        orders(near), near, momentum, gradient, left_own, left_other, q_own, q_other
    )
    *q_own[2], _ = lax.optimization_barrier((*q_own[2], new_momentum))
    q_other[2] = [swap_cores(part) for part in q_own[2]]
    squares = sum_squares([part for parts in q_own for part in parts]).reshape(HALF)
    basis_scale = lax.rsqrt(squared * squares + EPSILON)
    factors = jnp.stack([squared * basis_scale, scale * basis_scale])
    factors_other = swap_cores(factors)

    def place_of(unit):
        dx, dy = (unit // 4 - x) % 4, ((unit % 2) * 2 + (unit // 2) % 2 - y) % 4
        return [jnp.where(first, dx, dy), jnp.where(first, dy, dx)]

    block = (row % 4) * 4 + row // 4
    place = place_of(col) + place_of(block) + place_of(block + 2) + [core]
    step_scale = STEP_SIZE * math.sqrt(total_rows * width / rank)
    factors, factors_other = factors * jnp.array([[step_scale], [1.0]], F32), factors_other * jnp.array(
        [[step_scale], [1.0]], F32
    )
    tile = [
        new_momentum,
        jnp.stack(place).astype(jnp.int32),
        jnp.stack([factors[0], factors_other[0], factors[1], factors_other[1]]),
        early,
        mine,
        theirs,
        weight,
        p_tile,
        p_tile_other,
        total_rows ** (-0.5),
    ]
    new_momentum, new_weight, logits, new_basis = update_momentum(
        orders(across), across, momentum, gradient, left_own, left_other, q_own, q_other, tile
    )
    return (new_momentum, new_basis, new_weight, logits)


def solution(mesh):
    in_specs = (
        P(("row", "col"), None),
        P(("row", "col"), None),
        P(("row", "col"), None),
        P("row", "col"),
        P("col", "row"),
    )
    out_specs = (P(("row", "col"), None), P(("row", "col"), None), P("row", "col"), P("row", "col"))
    return jax.shard_map(shards, mesh=mesh, in_specs=in_specs, out_specs=out_specs, check_vma=False)
```
